32 devices in a mesh: tm: 4 (over z), seq: 8 (over y, x, core).
Axes of the slice: x: 2, y: 2, z: 4, core: 2. Of those that a mesh axis runs over, the one named last changes fastest.
Arguments:
- states: float32 [32, 384, 64], P('tm', 'seq'), may hold values from -11 to 11
- first_state: float32 [384, 64], P('seq'), may hold values from -6 to 6
- now_step: int32 [32], P('tm'), may hold values from 1 to 960, as said below
- next_step: int32 [32], P('tm'), may hold values from 0 to 959, as said below
- embed_weight: bfloat16 [64, 1536], replicated, may hold values from -0.75 to 0.75
- mod_weight: bfloat16 [256, 4608], replicated, may hold values from -0.375 to 0.375
- qkv_weight: bfloat16 [1536, 12, 384], P('seq'), may hold values from -1 to 1
- out_weight: bfloat16 [1536, 1536], P('seq'), may hold values from -0.15625 to 0.15625
- final_weight: bfloat16 [1536, 64], replicated, may hold values from -0.15625 to 0.15625
Outputs:
- advanced: float32 [32, 384, 64], P('tm', 'seq')
- errors: float32 [32], P('tm')
The draws below stay inside these ranges and needn't reach their ends.
Inputs may be any that keep to these rules, and one draw needn't show every extreme that they name: now_step[0] = 960 and now_step[j + 1] = next_step[j]. next_step[j] is now_step[j] minus a gap of 1 to 30.
All inputs are finite; a program needn't handle non-finite values.
Results may differ from the reference program's by a relative error of at most 0.002.
Values may be sent and summed in bfloat16 or wider, within the bound.
No kernel may reach another device: no remote copies, remote signals or barrier semaphores. Data moves between devices by JAX's collectives and lax.ppermute only.
A program may use at most 64 MiB of HBM per device.

```python
import math
import jax
import jax.numpy as jnp
from jax import lax

D = 1536
HEADS = 12
FREQ = 256
HD = 128
CH = 64
L = 384
WIN = 32


def plan_gaps(key):
    largest_gap = 960 // WIN
    return jax.random.randint(jax.random.fold_in(key, 7), (WIN,), 1, largest_gap + 1)


def draw_now_step(key, part):
    step_gaps = plan_gaps(key)
    return (960 - jnp.cumsum(step_gaps) + step_gaps).astype(jnp.int32)


def draw_next_step(key, part):
    step_gaps = plan_gaps(key)
    return (960 - jnp.cumsum(step_gaps)).astype(jnp.int32)


def draw_states(key, part):
    value_key = jax.random.fold_in(key, 21)
    jitter_key = jax.random.fold_in(key, 22)
    position = jnp.arange(L, dtype=jnp.float32) / max(L - 1, 1)
    jitter = jnp.exp(jax.random.uniform(jitter_key, (WIN, L, 1), jnp.float32, math.log(0.7), math.log(1.4)))
    token_ramp = 0.6 + 1.2 * position
    entries = jnp.clip(jax.random.normal(value_key, (WIN, L, CH), jnp.float32), -4.0, 4.0)
    return entries * token_ramp[None, :, None] * jitter


def draw_qkv_weight(key, part):
    entries = jnp.clip(jax.random.normal(jax.random.fold_in(key, 31), (D, HEADS, 3 * HD), jnp.float32), -4.0, 4.0) * D ** (-0.5)
    return jnp.clip(entries, -1.0, 1.0).astype(jnp.bfloat16)


def levels(own_key, extent, pieces, low, largest):
    gain = 1.0
    for dim, blocks in pieces:
        steps = jax.random.uniform(jax.random.fold_in(jax.random.fold_in(own_key, 6), dim), (blocks,), jnp.float32, low / len(pieces), largest / len(pieces))
        gain = gain * jnp.repeat(jnp.exp(steps), extent[dim] // blocks).reshape((-1,) + (1,) * (len(extent) - 1 - dim))
    return gain


def bell_draw(rng, dims, deviation, bound, shards=(), held_as=jnp.bfloat16):
    array = deviation * jax.random.normal(rng, dims, jnp.float32)
    if shards:
        array = array * levels(rng, dims, shards, -0.22, 0.18)
    return jnp.clip(array, -bound, bound).astype(held_as)


def setup_inputs(seed: int = 0) -> dict:
    key_of = jax.random.split(jax.random.key(seed), 10)
    states = draw_states(jax.random.fold_in(key_of[9], 71), 0)
    first_state = bell_draw(key_of[1], (L, CH), 1.0, 6.0, ((0, 8),), jnp.float32)
    now_step = draw_now_step(jax.random.fold_in(key_of[9], 71), 0)
    next_step = draw_next_step(jax.random.fold_in(key_of[9], 71), 0)
    embed_weight = bell_draw(key_of[4], (CH, D), CH ** -0.5, 0.75)
    mod_weight = bell_draw(key_of[5], (FREQ, 3 * D), FREQ ** -0.5, 0.375)
    qkv_weight = draw_qkv_weight(jax.random.fold_in(key_of[9], 71), 0)
    out_weight = bell_draw(key_of[7], (D, D), D ** -0.5, 0.15625, ((0, 8),))
    final_weight = bell_draw(key_of[8], (D, CH), D ** -0.5, 0.15625)
    return {"states": states, "first_state": first_state, "now_step": now_step, "next_step": next_step, "embed_weight": embed_weight, "mod_weight": mod_weight, "qkv_weight": qkv_weight, "out_weight": out_weight, "final_weight": final_weight}


def layer_norm(rows):
    row_mean = lax.optimization_barrier(jnp.mean(rows, axis=-1, keepdims=True))
    centered = rows - row_mean
    variance = lax.optimization_barrier(jnp.mean(centered * centered, axis=-1, keepdims=True))
    return centered * lax.rsqrt(variance + 1e-06)

def alpha_bar(step_ids):
    fraction = (step_ids.astype(jnp.float32) / 1000.0 + 0.008) / 1.008
    return jnp.cos(fraction * (math.pi / 2)) ** 2

def coefficients(now_step, next_step):
    alpha_now = alpha_bar(now_step)
    alpha_next = alpha_bar(next_step)
    step_ratio = jnp.sqrt(alpha_next / alpha_now)
    keep_coef = step_ratio - 1.0
    noise_coef = jnp.sqrt(1.0 - alpha_next) - step_ratio * jnp.sqrt(1.0 - alpha_now)
    return (keep_coef, noise_coef)

def modulation(step_ids, mod_weight):
    half_freq = mod_weight.shape[0] // 2
    frequency = jnp.exp(-math.log(10000.0) * jnp.arange(half_freq, dtype=jnp.float32) / half_freq)
    angles = step_ids.astype(jnp.float32)[:, None] * frequency[None, :]
    time_embed = jnp.concatenate([jnp.cos(angles), jnp.sin(angles)], axis=1).astype(jnp.bfloat16)
    return jnp.dot(time_embed, mod_weight, preferred_element_type=jnp.float32)

def attend_one(pair_item):
    hdim = pair_item.shape[1] // 3
    length = pair_item.shape[0]
    query_rows = 512 if length % 512 == 0 else length
    queries = pair_item[:, :hdim]
    key_rows = pair_item[:, hdim:2 * hdim]
    values = pair_item[:, 2 * hdim:]

    def one_block(query_block):
        scores = jnp.dot(query_block, key_rows.T, preferred_element_type=jnp.float32) * hdim ** (-0.5)
        row_max = lax.optimization_barrier(jnp.max(scores, axis=1, keepdims=True))
        exponent = jnp.exp(scores - row_max)
        weights = (exponent / lax.optimization_barrier(jnp.sum(exponent, axis=1, keepdims=True))).astype(jnp.bfloat16)
        return jnp.dot(weights, values, preferred_element_type=jnp.float32).astype(jnp.bfloat16)
    blocks_out = lax.map(one_block, queries.reshape(length // query_rows, query_rows, hdim))
    return blocks_out.reshape(length, hdim)

def reference(states, first_state, now_step, next_step, embed_weight, mod_weight, qkv_weight, out_weight, final_weight):
    previous = jnp.concatenate([first_state[None], states[:-1]], axis=0)
    keep_coef, noise_coef = coefficients(now_step, next_step)
    modulated_all = modulation(now_step, mod_weight)

    def one_step(inputs):
        prev_state, mod_row = inputs
        shift_mod = mod_row[:D]
        scale_mod = mod_row[D:2 * D]
        gate_mod = mod_row[2 * D:]
        residual = jnp.dot(prev_state.astype(jnp.bfloat16), embed_weight, preferred_element_type=jnp.float32)
        modulated = (layer_norm(residual) * (1.0 + scale_mod[None, :]) + shift_mod[None, :]).astype(jnp.bfloat16)
        projected = jnp.dot(modulated, qkv_weight.reshape(D, HEADS * 3 * HD), preferred_element_type=jnp.float32)
        projected = projected.astype(jnp.bfloat16).reshape(L, HEADS, 3 * HD)
        heads_out = lax.map(attend_one, jnp.transpose(projected, (1, 0, 2)))
        flattened = jnp.transpose(heads_out, (1, 0, 2)).reshape(L, D)
        projection = jnp.dot(flattened, out_weight, preferred_element_type=jnp.float32)
        updated = residual + gate_mod[None, :] * projection
        normed_out = layer_norm(updated).astype(jnp.bfloat16)
        return jnp.dot(normed_out, final_weight, preferred_element_type=jnp.float32)
    noise_pred = lax.map(one_step, (previous, modulated_all))
    drift_terms = keep_coef[:, None, None] * previous + noise_coef[:, None, None] * noise_pred
    advanced = first_state[None] + jnp.cumsum(drift_terms, axis=0)
    difference = advanced - states
    errors = lax.optimization_barrier(jnp.mean(difference * difference, axis=(1, 2)))
    return (advanced, errors)
```

```python
import functools
import math

import jax
import jax.numpy as jnp
from jax import lax
from jax.experimental import pallas as pl
from jax.experimental.pallas import tpu as pltpu
from jax.sharding import PartitionSpec as P

BF = jnp.bfloat16
F32 = jnp.float32
ROWS = 80
VMEM_LIMIT = 48 * 1024 * 1024


def dot(a, b, dims=((1,), (0,))):
    return lax.dot_general(a, b, (dims, ((), ())), preferred_element_type=F32)


def alpha_bar(step_ids):
    fraction = (step_ids.astype(F32) / 1000.0 + 0.008) / 1.008
    return jnp.cos(fraction * (math.pi / 2)) ** 2


def coefficients(now_step, next_step):
    alpha_now = alpha_bar(now_step)
    alpha_next = alpha_bar(next_step)
    step_ratio = jnp.sqrt(alpha_next / alpha_now)
    keep_coef = step_ratio - 1.0
    noise_coef = jnp.sqrt(1.0 - alpha_next) - step_ratio * jnp.sqrt(1.0 - alpha_now)
    return (keep_coef, noise_coef)


def modulation(step_ids, mod_weight):
    half_freq = mod_weight.shape[0] // 2
    frequency = jnp.exp(-math.log(10000.0) * jnp.arange(half_freq, dtype=F32) / half_freq)
    angles = step_ids.astype(F32)[:, None] * frequency[None, :]
    time_embed = jnp.concatenate([jnp.cos(angles), jnp.sin(angles)], axis=1).astype(BF)
    return jnp.dot(time_embed, mod_weight, preferred_element_type=F32)


def prepare_kernel(steps, per, sub, embed_ref, mod_ref, w_ref, out_ref, b_scr):
    chans, width = embed_ref.shape
    embed = embed_ref[...].astype(F32)
    centred = embed - jnp.mean(embed, axis=1, keepdims=True)
    pad = jnp.zeros((ROWS - chans - 8, width), F32)
    first = lax.broadcasted_iota(jnp.int32, (8, width), 0) == 0
    for t in range(steps):
        shift = mod_ref[t : t + 1, :width]
        scale = mod_ref[t : t + 1, width : 2 * width]
        tail = jnp.where(first, jnp.broadcast_to(shift, (8, width)), 0.0)
        rows = jnp.concatenate([centred * (1.0 + scale), tail, pad], axis=0)
        b_scr[t * ROWS : (t + 1) * ROWS, :] = rows.astype(BF)
    cols = per * sub
    a_all = dot(b_scr[...], w_ref[...]).astype(BF)
    for t in range(steps):
        a_t = a_all[t * ROWS : (t + 1) * ROWS]
        for i in range(per):
            q = a_t[:, i * sub : (i + 1) * sub]
            k = a_t[:, cols + i * sub : cols + (i + 1) * sub]
            prod = dot(q, k, ((1,), (1,)))
            out_ref[t, :, i * chans : (i + 1) * chans] = prod[:, :chans].astype(BF)
        out_ref[t, :, per * chans :] = a_t[:, 2 * cols :]


def prepare(embed, mod_all, w_mine, steps, per, sub):
    chans = embed.shape[0]
    return pl.pallas_call(
        functools.partial(prepare_kernel, steps, per, sub),
        out_shape=jax.ShapeDtypeStruct((steps, ROWS, per * (chans + sub)), BF),
        scratch_shapes=[pltpu.VMEM((steps * ROWS, embed.shape[1]), BF)],
        compiler_params=pltpu.CompilerParams(vmem_limit_bytes=VMEM_LIMIT),
        name="prepare",
    )(embed, mod_all, w_mine)


def attend_kernel(heads, n_sub, per, sub, embed_ref, keys_ref, queries_ref, pay_ref, out_ref):
    chans, width = embed_ref.shape
    hdim = n_sub * sub
    embed = embed_ref[...].astype(F32)
    centred = embed - jnp.mean(embed, axis=1, keepdims=True)
    centred = centred.astype(BF)

    def inverse_dev(p):
        rows = dot(p, embed_ref[...])
        mean = jnp.mean(rows, axis=1, keepdims=True)
        rows = rows - mean
        return lax.rsqrt(jnp.mean(rows * rows, axis=1, keepdims=True) + 1e-6)

    keys = keys_ref[...]
    keys_t = keys.astype(F32).T.astype(BF)
    queries = queries_ref[...]
    key_dev = inverse_dev(keys)
    query_dev = inverse_dev(queries)
    factor = hdim**-0.5 * math.log2(math.e)
    halves = []
    for h in range(heads):
        product = None
        value_parts = []
        for j in range(n_sub):
            source, slot = divmod(h * n_sub + j, per)
            part = pay_ref[source, :, slot * chans : (slot + 1) * chans].astype(F32)
            product = part if product is None else product + part
            start = per * chans + slot * sub
            value_parts.append(pay_ref[source, :, start : start + sub])
        value = jnp.concatenate(value_parts, axis=1) if n_sub > 1 else value_parts[0]
        side = dot(queries, product[:chans].astype(BF)) * query_dev + product[chans : chans + 1]
        side = (side * factor).astype(BF)
        scores = dot(keys, side, ((1,), (1,))) * key_dev
        top = jnp.max(scores, axis=0, keepdims=True)
        weights = jnp.exp2(scores - top)
        total = jnp.sum(weights, axis=0, keepdims=True)
        mixed = dot(keys_t, (weights * key_dev).astype(BF)) / total
        mixed = mixed.T.astype(BF)
        result = dot(mixed, value[:chans]) + value[chans : chans + 1].astype(F32)
        out_ref[:, h * hdim : (h + 1) * hdim] = result.astype(BF)


def attend(embed, keys, queries, payload, heads, n_sub, per, sub):
    return pl.pallas_call(
        functools.partial(attend_kernel, heads, n_sub, per, sub),
        out_shape=jax.ShapeDtypeStruct((queries.shape[0], heads * n_sub * sub), BF),
        compiler_params=pltpu.CompilerParams(vmem_limit_bytes=VMEM_LIMIT),
        name="attend",
    )(embed, keys, queries, payload)


def finish_kernel(embed_ref, queries_ref, att_ref, wo_ref, gate_ref, final_ref, out_ref):
    residual = dot(queries_ref[...], embed_ref[...])
    updated = residual + gate_ref[...] * dot(att_ref[...], wo_ref[...])
    mean = jnp.mean(updated, axis=1, keepdims=True)
    centred = updated - mean
    variance = jnp.mean(centred * centred, axis=1, keepdims=True)
    normed = (centred * lax.rsqrt(variance + 1e-6)).astype(BF)
    out_ref[...] = dot(normed, final_ref[...])


def finish(embed, queries, att, wo, gate, final):
    return pl.pallas_call(
        finish_kernel,
        out_shape=jax.ShapeDtypeStruct((queries.shape[0], final.shape[1]), F32),
        compiler_params=pltpu.CompilerParams(vmem_limit_bytes=VMEM_LIMIT),
        name="finish",
    )(embed, queries, att, wo, gate, final)


def swap(x, mask, count):
    return lax.ppermute(x, "seq", [(i, i ^ mask) for i in range(count)])


def gather_rows(shard, count):
    if count != 8:
        return lax.all_gather(shard, "seq", axis=0, tiled=True)
    half = shard.shape[0] // 2
    a, b = shard[:half], shard[half:]
    xa, yb = swap(a, 2, count), swap(b, 4, count)
    ya, xya = swap(a, 4, count), swap(xa, 4, count)
    xb, xyb = swap(b, 2, count), swap(yb, 2, count)
    mine = jnp.stack([a, b, xa, xb, ya, yb, xya, xyb]).reshape(4, 2 * half, -1)
    other = swap(mine, 1, count)
    index = lax.axis_index("seq")
    core, chip = index % 2, index // 2
    first = jnp.where(core == 0, mine, other)
    second = jnp.where(core == 0, other, mine)
    pairs = jnp.stack([first, second], axis=1)
    order = jnp.arange(4) ^ chip
    return jnp.take(pairs, order, axis=0).reshape(count * shard.shape[0], -1)


def earlier_total(total, count):
    place = lax.axis_index("tm")
    carried = jnp.zeros_like(total)
    for by in range(1, count):
        carried += lax.ppermute(total, "tm", [(i, i + by) for i in range(count - by)])
    return carried


def per_device(
    states,
    first_state,
    now_step,
    next_step,
    embed_weight,
    mod_weight,
    qkv_weight,
    out_weight,
    final_weight,
):
    steps, tokd, chans = states.shape
    count = lax.axis_size("seq")
    tm_count = lax.axis_size("tm")
    time_index = lax.axis_index("tm")
    seq_index = lax.axis_index("seq")
    rows, heads, width_three = qkv_weight.shape
    hdim = width_three // 3
    width = heads * hdim
    share = count // steps
    n_sub = count // math.gcd(count, heads)
    per = heads * n_sub // count
    sub = hdim // n_sub

    w = qkv_weight.reshape(rows, heads, 3, n_sub, sub)
    w = w.transpose(1, 3, 0, 2, 4).reshape(count, per, rows, 3, sub)
    w = w.transpose(0, 2, 3, 1, 4).reshape(count, rows, 3 * per * sub)
    w_mine = lax.all_to_all(w, "seq", 0, 0, tiled=True).reshape(count * rows, 3 * per * sub)
    wo = gather_rows(out_weight, count)

    edge = lax.ppermute(states[-1], "tm", [(i, i + 1) for i in range(tm_count - 1)])
    opening = jnp.where(time_index == 0, first_state, edge)
    previous = jnp.concatenate([opening[None], states[:-1]], axis=0)
    sent = jnp.repeat(previous.astype(BF), share, axis=0)
    keys = lax.all_to_all(sent, "seq", 0, 0, tiled=True).reshape(count * tokd, chans)
    length = count * tokd // share
    mine = seq_index // share
    part = seq_index % share
    queries = lax.dynamic_slice_in_dim(keys, part * length, length, 0) if share > 1 else keys

    keep_coef, noise_coef = coefficients(now_step, next_step)
    mod_all = modulation(now_step, mod_weight)
    payload = prepare(embed_weight, mod_all, w_mine, steps, per, sub)
    payload = jnp.repeat(payload, share, axis=0)
    payload = lax.all_to_all(payload, "seq", 0, 0, tiled=True)
    att = attend(embed_weight, keys, queries, payload, heads, n_sub, per, sub)
    gate = lax.dynamic_slice(mod_all, (mine, 2 * width), (1, width))
    noise = finish(embed_weight, queries, att, wo, gate, final_weight)

    noise = noise.reshape(count // share, tokd, chans)
    if share > 1:
        full = jnp.zeros((share,) + noise.shape, F32)
        noise = lax.dynamic_update_slice(full, noise[None], (part, 0, 0, 0))
        noise = noise.reshape(count, tokd, chans)
    noise = lax.all_to_all(noise, "seq", 0, 0, tiled=True)
    if share > 1:
        noise = noise.reshape(steps, share, tokd, chans)
        own = seq_index // (count // share)
        noise = lax.dynamic_index_in_dim(noise, own, 1, False)

    drift_terms = keep_coef[:, None, None] * previous + noise_coef[:, None, None] * noise
    running_sums = jnp.cumsum(drift_terms, axis=0)
    carried = earlier_total(running_sums[-1], tm_count)
    advanced = first_state[None] + carried[None] + running_sums
    difference = advanced - states
    partial_value = jnp.sum(difference * difference, axis=(1, 2))
    errors = lax.psum(partial_value, "seq") / (tokd * count * chans)
    return (advanced, errors)


def solution(mesh):
    in_specs = (
        P("tm", "seq", None),
        P("seq", None),
        P("tm"),
        P("tm"),
        P(),
        P(),
        P("seq", None, None),
        P("seq", None),
        P(),
    )
    out_specs = (P("tm", "seq", None), P("tm"))
    return jax.shard_map(
        per_device, mesh=mesh, in_specs=in_specs, out_specs=out_specs, check_vma=False
    )
```

```python
import functools
import math

import jax
import jax.numpy as jnp
from jax import lax
from jax.experimental import pallas as pl
from jax.experimental.pallas import tpu as pltpu
from jax.sharding import PartitionSpec as P

BF = jnp.bfloat16
F32 = jnp.float32
ROWS = 80
MIB = 1024 * 1024


def dot(a, b, dims=((1,), (0,))):
    return lax.dot_general(a, b, (dims, ((), ())), preferred_element_type=F32)


def alpha_bar(step_ids):
    fraction = (step_ids.astype(F32) / 1000.0 + 0.008) / 1.008
    return jnp.cos(fraction * (math.pi / 2)) ** 2


def coefficients(now_step, next_step):
    alpha_now = alpha_bar(now_step)
    alpha_next = alpha_bar(next_step)
    step_ratio = jnp.sqrt(alpha_next / alpha_now)
    keep_coef = step_ratio - 1.0
    noise_coef = jnp.sqrt(1.0 - alpha_next) - step_ratio * jnp.sqrt(1.0 - alpha_now)
    return (keep_coef, noise_coef)


def modulation(step_ids, mod_weight):
    half_freq = mod_weight.shape[0] // 2
    frequency = jnp.exp(-math.log(10000.0) * jnp.arange(half_freq, dtype=F32) / half_freq)
    angles = step_ids.astype(F32)[:, None] * frequency[None, :]
    time_embed = jnp.concatenate([jnp.cos(angles), jnp.sin(angles)], axis=1).astype(BF)
    return jnp.dot(time_embed, mod_weight, preferred_element_type=F32)


SMEM = pl.BlockSpec(memory_space=pltpu.SMEM)
VMEM = pl.BlockSpec(memory_space=pltpu.VMEM)


def params(mib):
    return pltpu.CompilerParams(vmem_limit_bytes=mib * MIB)


def cut_kernel(n_sub, per, sub, w_ref, out_ref):
    for dest in range(out_ref.shape[0]):
        pieces = []
        for kind in (0, 2, 1):
            for i in range(per):
                head, part = divmod(dest * per + i, n_sub)
                start = kind * n_sub * sub + part * sub
                pieces.append(w_ref[head, :, start : start + sub])
        out_ref[dest] = jnp.concatenate(pieces, axis=1)


def cut(w, count, n_sub, per, sub):
    return pl.pallas_call(
        functools.partial(cut_kernel, n_sub, per, sub),
        out_shape=jax.ShapeDtypeStruct((count, w.shape[1], 3 * per * sub), BF),
        compiler_params=params(8),
        name="cut",
    )(w)


def prepare_kernel(per, sub, embed_ref, mod_ref, w_ref, states_ref, opening_ref, out_ref, basis_scr):
    steps, tokd, chans = states_ref.shape
    width = embed_ref.shape[1]
    embed = embed_ref[...].astype(F32)
    centred = embed - jnp.mean(embed, axis=1, keepdims=True)
    pad = jnp.zeros((ROWS - chans - 8, width), F32)
    first = lax.broadcasted_iota(jnp.int32, (8, width), 0) == 0
    for t in range(steps):
        shift = mod_ref[t : t + 1, :width]
        scale = mod_ref[t : t + 1, width : 2 * width]
        tail = jnp.where(first, jnp.broadcast_to(shift, (8, width)), 0.0)
        rows = jnp.concatenate([centred * (1.0 + scale), tail, pad], axis=0)
        basis_scr[t * ROWS : (t + 1) * ROWS, :] = rows.astype(BF)
    cols = per * sub
    row = lax.broadcasted_iota(jnp.int32, (per * chans, cols), 0) // chans
    lane = lax.broadcasted_iota(jnp.int32, (per * chans, cols), 1) // sub
    same = row == lane
    body = per * (chans + sub)
    values = lax.broadcasted_iota(jnp.int32, (ROWS, body), 1) >= per * chans
    half = steps // 2 * ROWS
    sides = [dot(basis_scr[:half, :], w_ref[...]), dot(basis_scr[half:, :], w_ref[...])]
    for t in range(steps):
        start = t * ROWS % half
        a_t = sides[t * ROWS // half][start : start + ROWS]
        k = jnp.concatenate([a_t[:chans, 2 * cols :].astype(BF)] * per, axis=0)
        k = jnp.where(same, k, jnp.zeros_like(k))
        product = dot(a_t[:, :cols].astype(BF), k, ((1,), (1,)))
        if sub == chans:
            product = jnp.concatenate([product, product], axis=1)
            block = jnp.where(values, a_t[:, : 2 * cols], product)
        else:
            block = jnp.concatenate([product, a_t[:, cols : 2 * cols]], axis=1)
        before = opening_ref if t == 0 else states_ref.at[t - 1]
        groups = [before[i : i + 8, :] for i in range(0, tokd, 8)]
        last = jnp.concatenate(groups, axis=1)
        low = block[ROWS - 16 : ROWS - 8]
        if last.shape[1] > body:
            low = jnp.concatenate([low, jnp.zeros((8, last.shape[1] - body), F32)], axis=1)
        out_ref[t, : ROWS - 16, :body] = block[: ROWS - 16].astype(BF)
        out_ref[t, ROWS - 16 :, :] = jnp.concatenate([low, last], axis=0).astype(BF)


def prepare(embed, mod_all, w_mine, states, opening, per, sub):
    steps, tokd, chans = states.shape
    lanes = max(per * (chans + sub), tokd // 8 * chans)
    return pl.pallas_call(
        functools.partial(prepare_kernel, per, sub),
        out_shape=jax.ShapeDtypeStruct((steps, ROWS, lanes), BF),
        scratch_shapes=[pltpu.VMEM((steps * ROWS, embed.shape[1]), BF)],
        compiler_params=params(16),
        name="prepare",
    )(embed, mod_all, w_mine, states, opening)


def attend_kernel(
    heads, n_sub, per, sub, tokd, part_ref, embed_ref, pay_ref, out_ref, queries_ref, keys_scr
):
    chans = embed_ref.shape[0]
    hdim = n_sub * sub
    length = queries_ref.shape[0]
    for source in range(pay_ref.shape[0]):
        last = pay_ref[source, ROWS - 16 :, :].astype(F32)[8:]
        for i in range(tokd // 8):
            start = source * tokd + i * 8
            keys_scr[start : start + 8, :] = last[:, i * chans : (i + 1) * chans]
    first = pl.multiple_of(part_ref[0] * length, length)

    def augmented(p):
        residual = dot(p.astype(BF), embed_ref[...])
        residual = residual - jnp.mean(residual, axis=1, keepdims=True)
        variance = jnp.mean(residual * residual, axis=1, keepdims=True)
        lane = lax.broadcasted_iota(jnp.int32, p.shape, 1)
        return jnp.concatenate([p * lax.rsqrt(variance + 1e-6), (lane == 0).astype(F32)], axis=1)

    every = augmented(keys_scr[...])
    queries = keys_scr[pl.ds(first, length), :]
    queries_ref[...] = queries.astype(BF)
    mine = every if length == keys_scr.shape[0] else augmented(queries)
    keys = every[:, :chans].astype(BF)
    every_t = every.T[: chans + 16].astype(BF)
    products, values = [], []
    for h in range(heads):
        product = None
        value_parts = []
        for j in range(n_sub):
            source, slot = divmod(h * n_sub + j, per)
            part = pay_ref[source, :, slot * chans : (slot + 1) * chans].astype(F32)
            product = part if product is None else product + part
            start = per * chans + slot * sub
            value_parts.append(pay_ref[source, :, start : start + sub])
        products.append(product.astype(BF))
        values.append(jnp.concatenate(value_parts, axis=1) if n_sub > 1 else value_parts[0])
    factor = hdim**-0.5 * math.log2(math.e)
    sides = (dot(mine[:, :ROWS].astype(BF), jnp.concatenate(products, axis=1)) * factor).astype(BF)

    def scores(h):
        return dot(keys, sides[:, h * chans : (h + 1) * chans], ((1,), (1,)))

    mixed = []
    now = scores(0)
    for h in range(heads):
        following = scores(h + 1) if h + 1 < heads else None
        weights = jnp.exp2(now - jnp.max(now, axis=0, keepdims=True)).astype(BF)
        rows = dot(every_t, weights)
        mixed.append(rows * (1.0 / rows[chans : chans + 1]))
        now = following
    for h in range(heads):
        result = dot(mixed[h].T.astype(BF), values[h])
        out_ref[:, h * hdim : (h + 1) * hdim] = result.astype(BF)


def attend(part, embed, payload, tokd, share, heads, n_sub, per, sub):
    length = payload.shape[0] * tokd
    return pl.pallas_call(
        functools.partial(attend_kernel, heads, n_sub, per, sub, tokd),
        out_shape=[
            jax.ShapeDtypeStruct((length // share, heads * n_sub * sub), BF),
            jax.ShapeDtypeStruct((length // share, embed.shape[0]), BF),
        ],
        in_specs=[SMEM, VMEM, VMEM],
        scratch_shapes=[pltpu.VMEM((length, embed.shape[0]), F32)],
        compiler_params=params(14 if share == 1 else 40),
        name="attend",
    )(part, embed, payload)


def finish_kernel(tokd, chip_ref, coef_ref, embed_ref, queries_ref, att_ref, gate_ref, final_ref, *refs):
    *wo_refs, out_ref = refs
    projection = None
    for i, ref in enumerate(wo_refs):
        if len(wo_refs) == 1:
            columns = att_ref[...]
        else:
            rows = ref.shape[0]
            start = pl.multiple_of(chip_ref[1 + i] * 2 * rows, 2 * rows)
            chip = att_ref[:, pl.ds(start, 2 * rows)]
            columns = jnp.where(chip_ref[0] == i % 2, chip[:, :rows], chip[:, rows:])
        term = dot(columns, ref[...])
        projection = term if projection is None else projection + term
    updated = dot(queries_ref[...], embed_ref[...]) + gate_ref[...] * projection
    centred = updated - jnp.mean(updated, axis=1, keepdims=True)
    variance = jnp.mean(centred * centred, axis=1, keepdims=True)
    normed = (centred * lax.rsqrt(variance + 1e-6)).astype(BF)
    noise = dot(normed, final_ref[...], ((1,), (1,))) * coef_ref[0]
    half = tokd // 2
    for i in range(out_ref.shape[1]):
        block = noise[i * tokd : (i + 1) * tokd]
        block = jnp.concatenate([block[:half], block[half:]], axis=1)
        for j in range(out_ref.shape[0]):
            out_ref[j, i] = block


def finish(chips, coef, embed, queries, att, gate, final, wo_parts, tokd, repeats):
    chans = final.shape[0]
    length = queries.shape[0]
    return pl.pallas_call(
        functools.partial(finish_kernel, tokd),
        out_shape=jax.ShapeDtypeStruct((repeats, length // tokd, tokd // 2, 2 * chans), F32),
        in_specs=[SMEM] * 2 + [VMEM] * (5 + len(wo_parts)),
        compiler_params=params(24),
        name="finish",
    )(chips, coef, embed, queries, att, gate, final, *wo_parts)


def advance_kernel(share, place_ref, keep_ref, noise_ref, states_ref, opening_ref, first_ref, kept_ref, out_ref, square_ref):
    groups, count = noise_ref.shape[:2]
    steps, tokd, chans = states_ref.shape
    packed = jnp.zeros(noise_ref.shape[2:], F32)
    for group in range(groups - 1):
        total = noise_ref[group, 0]
        for i in range(1, count):
            total = total + noise_ref[group, i]
        packed = packed + jnp.where(place_ref[0] > group, total, jnp.zeros_like(total))

    def unpack(x):
        return jnp.concatenate([x[:, :chans], x[:, chans:]], axis=0)

    state = first_ref[...] + kept_ref[...] + unpack(packed)
    for t in range(steps):
        noise = noise_ref[place_ref[0], t * share]
        for i in range(1, share):
            noise = noise + noise_ref[place_ref[0], t * share + i]
        before = opening_ref[...] if t == 0 else states_ref[t - 1]
        state = state + (keep_ref[t] * before + unpack(noise))
        out_ref[t] = state
        error = state - states_ref[t]
        square_ref[t : t + 1, :] = jnp.sum(error * error, axis=0, keepdims=True)


def advance(place, keep, noise, states, opening, first, kept, share):
    steps, _, chans = states.shape
    return pl.pallas_call(
        functools.partial(advance_kernel, share),
        out_shape=[
            jax.ShapeDtypeStruct(states.shape, F32),
            jax.ShapeDtypeStruct((steps, chans), F32),
        ],
        in_specs=[SMEM] * 2 + [VMEM] * 5,
        compiler_params=params(8),
        name="advance",
    )(place, keep, noise, states, opening, first, kept)


def swap(x, mask, count):
    return lax.ppermute(x, "seq", [(i, i ^ mask) for i in range(count)])


def turn_by_plane(x, count, tm_count, swapped=0):
    pairs = []
    for i in range(tm_count):
        for j in range(count):
            pairs.append((i * count + j, i * count + (j ^ (4 if (i + j + swapped) % 2 else 2))))
    return lax.ppermute(x, ("tm", "seq"), pairs)


def earlier_total(total, count):
    place = lax.axis_index("tm")
    carried = jnp.zeros_like(total)
    for by in range(1, count):
        carried += lax.ppermute(total, "tm", [(i, i + by) for i in range(count - by)])
    return carried


def total_over_seq(part, count):
    if count != 8:
        return lax.psum(part, "seq")
    part = part + swap(part, 1, count)
    return part + swap(part, 2, count) + swap(part, 4, count) + swap(part, 6, count)


def per_device(
    states,
    first_state,
    now_step,
    next_step,
    embed_weight,
    mod_weight,
    qkv_weight,
    out_weight,
    final_weight,
):
    steps, tokd, chans = states.shape
    count = lax.axis_size("seq")
    tm_count = lax.axis_size("tm")
    time_index = lax.axis_index("tm")
    seq_index = lax.axis_index("seq")
    rows, heads, width_three = qkv_weight.shape
    hdim = width_three // 3
    width = heads * hdim
    share = count // steps
    n_sub = count // math.gcd(count, heads)
    per = heads * n_sub // count
    sub = hdim // n_sub
    barrier = lax.optimization_barrier
    mine = seq_index // share
    part = seq_index % share

    w_sent = cut(jnp.transpose(qkv_weight, (1, 0, 2)), count, n_sub, per, sub)
    w_mine = lax.all_to_all(w_sent, "seq", 0, 0, tiled=True).reshape(count * rows, 3 * per * sub)

    by_planes = count == 8 and tm_count % 2 == 0
    late_states, own, _ = barrier((states, out_weight, w_sent))
    edge = lax.ppermute(late_states[-1], "tm", [(i, i + 1) for i in range(tm_count - 1)])
    opening = jnp.where(time_index == 0, first_state, edge)
    if by_planes:
        wo_first = turn_by_plane(own, count, tm_count)
    keep_coef, noise_coef = coefficients(now_step, next_step)
    kept = keep_coef[0] * opening + jnp.sum(keep_coef[1:, None, None] * states[:-1], axis=0)
    kept = earlier_total(kept, tm_count)
    mod_all = modulation(now_step, mod_weight)
    gate = lax.dynamic_slice(mod_all, (mine, 2 * width), (1, width))
    coef = lax.dynamic_slice(noise_coef, (mine,), (1,))
    w_mine, mod_all, opening, kept, gate, coef = barrier((w_mine, mod_all, opening, kept, gate, coef))

    payload = prepare(embed_weight, mod_all, w_mine, states, opening, per, sub)
    sent = jnp.repeat(payload, share, axis=0)
    received = lax.all_to_all(sent, "seq", 0, 0, tiled=True)
    if by_planes:
        own, first, _ = barrier((own, wo_first, payload))
        second = lax.ppermute(first, "tm", [(i, i ^ 1) for i in range(tm_count)])
        third = turn_by_plane(first, count, tm_count, 1)
        late_second, late_third, _ = barrier((second, third, received))
        wo_parts = [own, swap(own, 1, count), first, swap(first, 1, count)]
        wo_parts += [late_third, swap(late_third, 1, count)]
        wo_parts += [late_second, swap(late_second, 1, count)]
        chip = seq_index // 2
        one = jnp.where((seq_index + time_index) % 2 == 0, 1, 2)
        two = 3 - one
        chips = jnp.stack([seq_index % 2, chip, chip, chip ^ one, chip ^ two])
        chips = jnp.concatenate([chips, jnp.stack([chip ^ 3, chip ^ 3, chip ^ two, chip ^ one])])
    else:
        wo_parts = [lax.all_gather(out_weight, "seq", axis=0, tiled=True)]
        chips = jnp.zeros((2,), jnp.int32)
    part_place = jnp.full((1,), part, jnp.int32)
    att, queries = attend(part_place, embed_weight, received, tokd, share, heads, n_sub, per, sub)
    repeats = tm_count if share == 1 else 1
    noise = finish(
        chips, coef, embed_weight, queries, att, gate, final_weight.T, wo_parts, tokd, repeats
    )

    if share > 1:
        full = jnp.zeros((share,) + noise.shape[1:], F32)
        full = lax.dynamic_update_slice(full, noise, (part, 0, 0, 0))
        noise = jnp.broadcast_to(full[None], (tm_count,) + full.shape)
    block = noise.shape[-2:]
    noise = noise.reshape((tm_count * count,) + block)
    noise = lax.all_to_all(noise, ("tm", "seq"), 0, 0, tiled=True)
    noise = noise.reshape((tm_count, count) + block)
    time_place = jnp.full((1,), time_index, jnp.int32)
    advanced, squares = advance(time_place, keep_coef, noise, states, opening, first_state, kept, share)
    errors = jnp.sum(total_over_seq(squares, count), axis=1) / (tokd * count * chans)
    return (advanced, errors)


def solution(mesh):
    in_specs = (
        P("tm", "seq", None),
        P("seq", None),
        P("tm"),
        P("tm"),
        P(),
        P(),
        P("seq", None, None),
        P("seq", None),
        P(),
    )
    out_specs = (P("tm", "seq", None), P("tm"))
    return jax.shard_map(
        per_device, mesh=mesh, in_specs=in_specs, out_specs=out_specs, check_vma=False
    )
```

```python
import functools
import math

import jax
import jax.numpy as jnp
from jax import lax
from jax.experimental import pallas as pl
from jax.experimental.pallas import tpu as pltpu
from jax.sharding import PartitionSpec as P

BF = jnp.bfloat16
F32 = jnp.float32
ROWS = 80
MIB = 1024 * 1024


def dot(a, b, dims=((1,), (0,))):
    return lax.dot_general(a, b, (dims, ((), ())), preferred_element_type=F32)


def alpha_bar(step_ids):
    fraction = (step_ids.astype(F32) / 1000.0 + 0.008) / 1.008
    return jnp.cos(fraction * (math.pi / 2)) ** 2


def coefficients(now_step, next_step):
    alpha_now = alpha_bar(now_step)
    alpha_next = alpha_bar(next_step)
    step_ratio = jnp.sqrt(alpha_next / alpha_now)
    keep_coef = step_ratio - 1.0
    noise_coef = jnp.sqrt(1.0 - alpha_next) - step_ratio * jnp.sqrt(1.0 - alpha_now)
    return (keep_coef, noise_coef)


def modulation(step_ids, mod_weight):
    half_freq = mod_weight.shape[0] // 2
    frequency = jnp.exp(-math.log(10000.0) * jnp.arange(half_freq, dtype=F32) / half_freq)
    angles = step_ids.astype(F32)[:, None] * frequency[None, :]
    time_embed = jnp.concatenate([jnp.cos(angles), jnp.sin(angles)], axis=1).astype(BF)
    return jnp.dot(time_embed, mod_weight, preferred_element_type=F32)


SMEM = pl.BlockSpec(memory_space=pltpu.SMEM)
VMEM = pl.BlockSpec(memory_space=pltpu.VMEM)


def params(mib):
    return pltpu.CompilerParams(vmem_limit_bytes=mib * MIB)


def packing(rows, lanes):
    main = lanes // 128 * 128
    rest = lanes - main
    if rest == 0:
        return (main, 0, 1, 0)
    each = main // rest
    return (main, rest, each, -(-(rows // 16) // each))


def cut_kernel(n_sub, per, sub, w_ref, out_ref):
    for dest in range(out_ref.shape[0]):
        pieces = []
        for kind in (0, 2, 1):
            for i in range(per):
                head, part = divmod(dest * per + i, n_sub)
                start = kind * n_sub * sub + part * sub
                pieces.append(w_ref[head, :, start : start + sub])
        block = jnp.concatenate(pieces, axis=1)
        rows, lanes = block.shape
        main, rest, each, strips = packing(rows, lanes)
        out_ref[dest, :rows, :] = block[:, :main]
        groups = [block[i : i + 16, main:] for i in range(0, rows, 16) if rest]
        groups += [jnp.zeros((16, rest), BF)] * (strips * each - len(groups))
        for i in range(strips):
            strip = jnp.concatenate(groups[i * each : (i + 1) * each], axis=1)
            out_ref[dest, rows + 16 * i : rows + 16 * (i + 1), :] = strip


def cut(w, count, n_sub, per, sub):
    main, _, _, strips = packing(w.shape[1], 3 * per * sub)
    return pl.pallas_call(
        functools.partial(cut_kernel, n_sub, per, sub),
        out_shape=jax.ShapeDtypeStruct((count, w.shape[1] + 16 * strips, main), BF),
        compiler_params=params(6),
        name="cut",
    )(w)


def prepare_kernel(
    per, sub, embed_ref, mod_ref, w_ref, states_ref, opening_ref, out_ref, basis_scr, rest_scr
):
    steps, tokd, chans = states_ref.shape
    width = embed_ref.shape[1]
    embed = embed_ref[...].astype(F32)
    centred = embed - jnp.mean(embed, axis=1, keepdims=True)
    pad = jnp.zeros((ROWS - chans - 8, width), F32)
    first = lax.broadcasted_iota(jnp.int32, (8, width), 0) == 0
    for t in range(steps):
        shift = mod_ref[t : t + 1, :width]
        scale = mod_ref[t : t + 1, width : 2 * width]
        tail = jnp.where(first, jnp.broadcast_to(shift, (8, width)), 0.0)
        rows = jnp.concatenate([centred * (1.0 + scale), tail, pad], axis=0)
        basis_scr[t * ROWS : (t + 1) * ROWS, :] = rows.astype(BF)
    cols = per * sub
    row = lax.broadcasted_iota(jnp.int32, (per * chans, cols), 0) // chans
    lane = lax.broadcasted_iota(jnp.int32, (per * chans, cols), 1) // sub
    same = row == lane
    body = per * (chans + sub)
    values = lax.broadcasted_iota(jnp.int32, (ROWS, body), 1) >= per * chans
    rows = width // w_ref.shape[0]
    main, rest, each, _ = packing(rows, 3 * cols)
    for source in range(w_ref.shape[0]):
        for i in range(rows // 16 if rest else 0):
            strip, j = divmod(i, each)
            group = w_ref[source, rows + 16 * strip : rows + 16 * (strip + 1), :]
            start = source * rows + 16 * i
            rest_scr[start : start + 16, :rest] = group[:, j * rest : (j + 1) * rest]
    whole = w_ref[:, :rows, :].reshape(width, main)
    half = steps // 2 * ROWS
    sides = []
    for start in (0, half):
        part = basis_scr[start : start + half, :]
        side = dot(part, whole)
        if rest:
            side = jnp.concatenate([side, dot(part, rest_scr[:, :rest])], axis=1)
        sides.append(side)
    for t in range(steps):
        start = t * ROWS % half
        a_t = sides[t * ROWS // half][start : start + ROWS]
        k = jnp.concatenate([a_t[:chans, 2 * cols :].astype(BF)] * per, axis=0)
        k = jnp.where(same, k, jnp.zeros_like(k))
        product = dot(a_t[:, :cols].astype(BF), k, ((1,), (1,)))
        if sub == chans:
            product = jnp.concatenate([product, product], axis=1)
            block = jnp.where(values, a_t[:, : 2 * cols], product)
        else:
            block = jnp.concatenate([product, a_t[:, cols : 2 * cols]], axis=1)
        before = opening_ref if t == 0 else states_ref.at[t - 1]
        groups = [before[i : i + 8, :] for i in range(0, tokd, 8)]
        last = jnp.concatenate(groups, axis=1)
        low = block[ROWS - 16 : ROWS - 8]
        if last.shape[1] > body:
            low = jnp.concatenate([low, jnp.zeros((8, last.shape[1] - body), F32)], axis=1)
        out_ref[t, : ROWS - 16, :body] = block[: ROWS - 16].astype(BF)
        out_ref[t, ROWS - 16 :, :] = jnp.concatenate([low, last], axis=0).astype(BF)


def prepare(embed, mod_all, w_mine, states, opening, per, sub):
    steps, tokd, chans = states.shape
    lanes = max(per * (chans + sub), tokd // 8 * chans)
    return pl.pallas_call(
        functools.partial(prepare_kernel, per, sub),
        out_shape=jax.ShapeDtypeStruct((steps, ROWS, lanes), BF),
        scratch_shapes=[
            pltpu.VMEM((steps * ROWS, embed.shape[1]), BF),
            pltpu.VMEM((embed.shape[1], 128), BF),
        ],
        compiler_params=params(10),
        name="prepare",
    )(embed, mod_all, w_mine, states, opening)


def attend_kernel(
    heads, n_sub, per, sub, tokd, part_ref, embed_ref, pay_ref, out_ref, queries_ref, keys_scr
):
    chans = embed_ref.shape[0]
    hdim = n_sub * sub
    length = queries_ref.shape[0]
    for source in range(pay_ref.shape[0]):
        last = pay_ref[source, ROWS - 16 :, :].astype(F32)[8:]
        for i in range(tokd // 8):
            start = source * tokd + i * 8
            keys_scr[start : start + 8, :] = last[:, i * chans : (i + 1) * chans]
    first = pl.multiple_of(part_ref[0] * length, length)

    def augmented(p):
        residual = dot(p.astype(BF), embed_ref[...])
        residual = residual - jnp.mean(residual, axis=1, keepdims=True)
        variance = jnp.mean(residual * residual, axis=1, keepdims=True)
        lane = lax.broadcasted_iota(jnp.int32, p.shape, 1)
        return jnp.concatenate([p * lax.rsqrt(variance + 1e-6), (lane == 0).astype(F32)], axis=1)

    every = augmented(keys_scr[...])
    queries = keys_scr[pl.ds(first, length), :]
    queries_ref[...] = queries.astype(BF)
    mine = every if length == keys_scr.shape[0] else augmented(queries)
    keys = every[:, :chans].astype(BF)
    every_t = every.T[: chans + 16].astype(BF)
    products, values = [], []
    for h in range(heads):
        product = None
        value_parts = []
        for j in range(n_sub):
            source, slot = divmod(h * n_sub + j, per)
            part = pay_ref[source, :, slot * chans : (slot + 1) * chans].astype(F32)
            product = part if product is None else product + part
            start = per * chans + slot * sub
            value_parts.append(pay_ref[source, :, start : start + sub])
        products.append(product.astype(BF))
        values.append(jnp.concatenate(value_parts, axis=1) if n_sub > 1 else value_parts[0])
    factor = hdim**-0.5 * math.log2(math.e)
    sides = (dot(mine[:, :ROWS].astype(BF), jnp.concatenate(products, axis=1)) * factor).astype(BF)

    def scores(h):
        return dot(keys, sides[:, h * chans : (h + 1) * chans], ((1,), (1,)))

    mixed = []
    now = scores(0)
    for h in range(heads):
        following = scores(h + 1) if h + 1 < heads else None
        weights = jnp.exp2(now - jnp.max(now, axis=0, keepdims=True)).astype(BF)
        rows = dot(every_t, weights)
        mixed.append(rows * (1.0 / rows[chans : chans + 1]))
        now = following
    for h in range(heads):
        result = dot(mixed[h].T.astype(BF), values[h])
        out_ref[:, h * hdim : (h + 1) * hdim] = result.astype(BF)


def attend(part, embed, payload, tokd, share, heads, n_sub, per, sub):
    length = payload.shape[0] * tokd
    return pl.pallas_call(
        functools.partial(attend_kernel, heads, n_sub, per, sub, tokd),
        out_shape=[
            jax.ShapeDtypeStruct((length // share, heads * n_sub * sub), BF),
            jax.ShapeDtypeStruct((length // share, embed.shape[0]), BF),
        ],
        in_specs=[SMEM, VMEM, VMEM],
        scratch_shapes=[pltpu.VMEM((length, embed.shape[0]), F32)],
        compiler_params=params(9 if share == 1 else 40),
        name="attend",
    )(part, embed, payload)


def finish_kernel(
    tokd, owner_ref, coef_ref, embed_ref, queries_ref, att_ref, gate_ref, final_ref, *refs
):
    *wo_refs, out_ref, wo_scr, sum_scr, sem = refs
    width = wo_scr.shape[1]
    chunk = width // 2
    copies = []
    for c in range(2):
        lanes = pl.ds(c * chunk, chunk)
        for i, ref in enumerate(wo_refs):
            rows = ref.shape[0]
            start = pl.multiple_of(owner_ref[i] * rows, rows)
            target = wo_scr.at[pl.ds(start, rows), lanes]
            copies.append(pltpu.make_async_copy(ref.at[:, lanes], target, sem.at[c, i]))
            copies[-1].start()
    total = 0.0
    for c in range(2):
        lanes = slice(c * chunk, (c + 1) * chunk)
        residual = dot(queries_ref[...], embed_ref[:, lanes])
        for copy in copies[c * len(wo_refs) : (c + 1) * len(wo_refs)]:
            copy.wait()
        updated = residual + gate_ref[:, lanes] * dot(att_ref[...], wo_scr[:, lanes])
        sum_scr[:, lanes] = updated
        total = total + jnp.sum(updated, axis=1, keepdims=True)
    centred = sum_scr[...] - total * (1.0 / width)
    variance = jnp.mean(centred * centred, axis=1, keepdims=True)
    normed = (centred * lax.rsqrt(variance + 1e-6)).astype(BF)
    noise = dot(normed, final_ref[...], ((1,), (1,))) * coef_ref[0]
    half = tokd // 2
    for i in range(out_ref.shape[1]):
        block = noise[i * tokd : (i + 1) * tokd]
        block = jnp.concatenate([block[:half], block[half:]], axis=1)
        for j in range(out_ref.shape[0]):
            out_ref[j, i] = block


def finish(owners, coef, embed, queries, att, gate, final, parts, tokd, repeats):
    chans, width = final.shape
    length = queries.shape[0]
    return pl.pallas_call(
        functools.partial(finish_kernel, tokd),
        out_shape=jax.ShapeDtypeStruct((repeats, length // tokd, tokd // 2, 2 * chans), F32),
        in_specs=[SMEM] * 2 + [VMEM] * 5 + [pl.BlockSpec(memory_space=pl.ANY)] * len(parts),
        scratch_shapes=[
            pltpu.VMEM((att.shape[1], width), BF),
            pltpu.VMEM((length, width), F32),
            pltpu.SemaphoreType.DMA((2, len(parts))),
        ],
        compiler_params=params(15),
        name="finish",
    )(owners, coef, embed, queries, att, gate, final, *parts)


def advance_kernel(share, place_ref, keep_ref, noise_ref, states_ref, opening_ref, first_ref, kept_ref, out_ref, square_ref):
    groups, count = noise_ref.shape[:2]
    steps, tokd, chans = states_ref.shape
    packed = jnp.zeros(noise_ref.shape[2:], F32)
    for group in range(groups - 1):
        total = noise_ref[group, 0]
        for i in range(1, count):
            total = total + noise_ref[group, i]
        packed = packed + jnp.where(place_ref[0] > group, total, jnp.zeros_like(total))

    def unpack(x):
        return jnp.concatenate([x[:, :chans], x[:, chans:]], axis=0)

    state = first_ref[...] + kept_ref[...] + unpack(packed)
    for t in range(steps):
        noise = noise_ref[place_ref[0], t * share]
        for i in range(1, share):
            noise = noise + noise_ref[place_ref[0], t * share + i]
        before = opening_ref[...] if t == 0 else states_ref[t - 1]
        state = state + (keep_ref[t] * before + unpack(noise))
        out_ref[t] = state
        error = state - states_ref[t]
        square_ref[t : t + 1, :] = jnp.sum(error * error, axis=0, keepdims=True)


def advance(place, keep, noise, states, opening, first, kept, share):
    steps, _, chans = states.shape
    return pl.pallas_call(
        functools.partial(advance_kernel, share),
        out_shape=[
            jax.ShapeDtypeStruct(states.shape, F32),
            jax.ShapeDtypeStruct((steps, chans), F32),
        ],
        in_specs=[SMEM] * 2 + [VMEM] * 5,
        compiler_params=params(4),
        name="advance",
    )(place, keep, noise, states, opening, first, kept)


def swap(x, mask, count):
    return lax.ppermute(x, "seq", [(i, i ^ mask) for i in range(count)])


def turn_by_plane(x, count, tm_count, swapped=0):
    pairs = []
    for i in range(tm_count):
        for j in range(count):
            pairs.append((i * count + j, i * count + (j ^ (4 if (i + j + swapped) % 2 else 2))))
    return lax.ppermute(x, ("tm", "seq"), pairs)


def earlier_total(total, count):
    place = lax.axis_index("tm")
    carried = jnp.zeros_like(total)
    for by in range(1, count):
        carried += lax.ppermute(total, "tm", [(i, i + by) for i in range(count - by)])
    return carried


def total_over_seq(part, count):
    if count != 8:
        return lax.psum(part, "seq")
    part = part + swap(part, 1, count)
    return part + swap(part, 2, count) + swap(part, 4, count) + swap(part, 6, count)


def per_device(
    states,
    first_state,
    now_step,
    next_step,
    embed_weight,
    mod_weight,
    qkv_weight,
    out_weight,
    final_weight,
):
    steps, tokd, chans = states.shape
    count = lax.axis_size("seq")
    tm_count = lax.axis_size("tm")
    time_index = lax.axis_index("tm")
    seq_index = lax.axis_index("seq")
    rows, heads, width_three = qkv_weight.shape
    hdim = width_three // 3
    width = heads * hdim
    share = count // steps
    n_sub = count // math.gcd(count, heads)
    per = heads * n_sub // count
    sub = hdim // n_sub
    barrier = lax.optimization_barrier
    mine = seq_index // share
    part = seq_index % share

    w_sent = cut(jnp.transpose(qkv_weight, (1, 0, 2)), count, n_sub, per, sub)
    w_mine = lax.all_to_all(w_sent, "seq", 0, 0, tiled=True)

    by_planes = count == 8 and tm_count % 2 == 0
    if by_planes:
        first = turn_by_plane(out_weight, count, tm_count)
    late_states, _ = barrier((states, w_sent))
    edge = lax.ppermute(late_states[-1], "tm", [(i, i + 1) for i in range(tm_count - 1)])
    opening = jnp.where(time_index == 0, first_state, edge)
    keep_coef, noise_coef = coefficients(now_step, next_step)
    kept = keep_coef[0] * opening + jnp.sum(keep_coef[1:, None, None] * states[:-1], axis=0)
    kept = earlier_total(kept, tm_count)
    mod_all = modulation(now_step, mod_weight)
    gate = lax.dynamic_slice(mod_all, (mine, 2 * width), (1, width))
    coef = lax.dynamic_slice(noise_coef, (mine,), (1,))
    if by_planes:
        late_first, _ = barrier((first, (kept, mod_all, gate, coef)))
        second = lax.ppermute(late_first, "tm", [(i, i ^ 1) for i in range(tm_count)])
    w_mine, mod_all, opening, kept, gate, coef = barrier((w_mine, mod_all, opening, kept, gate, coef))
    if by_planes:
        late_first, _ = barrier((first, w_mine))
        third = turn_by_plane(late_first, count, tm_count, 1)

    payload = prepare(embed_weight, mod_all, w_mine, states, opening, per, sub)
    sent = jnp.repeat(payload, share, axis=0)
    received = lax.all_to_all(sent, "seq", 0, 0, tiled=True)
    if by_planes:
        own, first, second, _ = barrier((out_weight, first, second, payload))
        third, _ = barrier((third, received))
        parts = []
        for block in (own, first, second, third):
            parts += [block, swap(block, 1, count)]
        one = jnp.where((seq_index + time_index) % 2 == 0, 2, 4)
        two = 6 - one
        zero = jnp.zeros_like(one)
        owners = [zero, zero + 1, one, two + 1, two, one + 1, zero + 6, zero + 7]
        owners = seq_index ^ jnp.stack(owners)
    else:
        parts = [lax.all_gather(out_weight, "seq", axis=0, tiled=True)]
        owners = jnp.zeros((1,), jnp.int32)
    part_place = jnp.full((1,), part, jnp.int32)
    att, queries = attend(part_place, embed_weight, received, tokd, share, heads, n_sub, per, sub)
    repeats = tm_count if share == 1 else 1
    noise = finish(
        owners, coef, embed_weight, queries, att, gate, final_weight.T, parts, tokd, repeats
    )

    if share > 1:
        full = jnp.zeros((share,) + noise.shape[1:], F32)
        full = lax.dynamic_update_slice(full, noise, (part, 0, 0, 0))
        noise = jnp.broadcast_to(full[None], (tm_count,) + full.shape)
    block = noise.shape[-2:]
    noise = noise.reshape((tm_count * count,) + block)
    noise = lax.all_to_all(noise, ("tm", "seq"), 0, 0, tiled=True)
    noise = noise.reshape((tm_count, count) + block)
    time_place = jnp.full((1,), time_index, jnp.int32)
    advanced, squares = advance(time_place, keep_coef, noise, states, opening, first_state, kept, share)
    errors = jnp.sum(total_over_seq(squares, count), axis=1) / (tokd * count * chans)
    return (advanced, errors)


def solution(mesh):
    in_specs = (
        P("tm", "seq", None),
        P("seq", None),
        P("tm"),
        P("tm"),
        P(),
        P(),
        P("seq", None, None),
        P("seq", None),
        P(),
    )
    out_specs = (P("tm", "seq", None), P("tm"))
    return jax.shard_map(
        per_device, mesh=mesh, in_specs=in_specs, out_specs=out_specs, check_vma=False
    )
```

```python
import functools
import math

import jax
import jax.numpy as jnp
from jax import lax
from jax.experimental import pallas as pl
from jax.experimental.pallas import tpu as pltpu
from jax.sharding import PartitionSpec as P

BF = jnp.bfloat16
F32 = jnp.float32
ROWS = 80
MIB = 1024 * 1024


def dot(a, b, dims=((1,), (0,))):
    return lax.dot_general(a, b, (dims, ((), ())), preferred_element_type=F32)


def alpha_bar(step_ids):
    fraction = (step_ids.astype(F32) / 1000.0 + 0.008) / 1.008
    return jnp.cos(fraction * (math.pi / 2)) ** 2


def coefficients(now_step, next_step):
    alpha_now = alpha_bar(now_step)
    alpha_next = alpha_bar(next_step)
    step_ratio = jnp.sqrt(alpha_next / alpha_now)
    keep_coef = step_ratio - 1.0
    noise_coef = jnp.sqrt(1.0 - alpha_next) - step_ratio * jnp.sqrt(1.0 - alpha_now)
    return (keep_coef, noise_coef)


def modulation(step_ids, mod_weight):
    half_freq = mod_weight.shape[0] // 2
    frequency = jnp.exp(-math.log(10000.0) * jnp.arange(half_freq, dtype=F32) / half_freq)
    angles = step_ids.astype(F32)[:, None] * frequency[None, :]
    time_embed = jnp.concatenate([jnp.cos(angles), jnp.sin(angles)], axis=1).astype(BF)
    return jnp.dot(time_embed, mod_weight, preferred_element_type=F32)


SMEM = pl.BlockSpec(memory_space=pltpu.SMEM)
VMEM = pl.BlockSpec(memory_space=pltpu.VMEM)


def params(mib):
    return pltpu.CompilerParams(vmem_limit_bytes=mib * MIB)


def packing(rows, lanes):
    main = lanes // 128 * 128
    rest = lanes - main
    if rest == 0:
        return (main, 0, 1, 0)
    each = main // rest
    return (main, rest, each, -(-(rows // 16) // each))


def cut_kernel(n_sub, per, sub, w_ref, out_ref):
    for dest in range(out_ref.shape[0]):
        pieces = []
        for kind in (0, 2, 1):
            for i in range(per):
                head, part = divmod(dest * per + i, n_sub)
                start = kind * n_sub * sub + part * sub
                pieces.append(w_ref[head, :, start : start + sub])
        block = jnp.concatenate(pieces, axis=1)
        rows, lanes = block.shape
        main, rest, each, strips = packing(rows, lanes)
        out_ref[dest, :rows, :] = block[:, :main]
        groups = [block[i : i + 16, main:] for i in range(0, rows, 16) if rest]
        groups += [jnp.zeros((16, rest), BF)] * (strips * each - len(groups))
        for i in range(strips):
            strip = jnp.concatenate(groups[i * each : (i + 1) * each], axis=1)
            out_ref[dest, rows + 16 * i : rows + 16 * (i + 1), :] = strip


def cut(w, count, n_sub, per, sub):
    main, _, _, strips = packing(w.shape[1], 3 * per * sub)
    return pl.pallas_call(
        functools.partial(cut_kernel, n_sub, per, sub),
        out_shape=jax.ShapeDtypeStruct((count, w.shape[1] + 16 * strips, main), BF),
        compiler_params=params(6),
        name="cut",
    )(w)


def prepare_kernel(
    per, sub, embed_ref, mod_ref, w_ref, states_ref, opening_ref, out_ref, basis_scr, rest_scr
):
    steps, tokd, chans = states_ref.shape
    width = embed_ref.shape[1]
    embed = embed_ref[...].astype(F32)
    centred = embed - jnp.mean(embed, axis=1, keepdims=True)
    pad = jnp.zeros((ROWS - chans - 8, width), F32)
    first = lax.broadcasted_iota(jnp.int32, (8, width), 0) == 0
    for t in range(steps):
        shift = mod_ref[t : t + 1, :width]
        scale = mod_ref[t : t + 1, width : 2 * width]
        tail = jnp.where(first, jnp.broadcast_to(shift, (8, width)), 0.0)
        rows = jnp.concatenate([centred * (1.0 + scale), tail, pad], axis=0)
        basis_scr[t * ROWS : (t + 1) * ROWS, :] = rows.astype(BF)
    cols = per * sub
    row = lax.broadcasted_iota(jnp.int32, (per * chans, cols), 0) // chans
    lane = lax.broadcasted_iota(jnp.int32, (per * chans, cols), 1) // sub
    same = row == lane
    body = per * (chans + sub)
    values = lax.broadcasted_iota(jnp.int32, (ROWS, body), 1) >= per * chans
    rows = width // w_ref.shape[0]
    main, rest, each, _ = packing(rows, 3 * cols)
    for source in range(w_ref.shape[0]):
        for i in range(rows // 16 if rest else 0):
            strip, j = divmod(i, each)
            group = w_ref[source, rows + 16 * strip : rows + 16 * (strip + 1), :]
            start = source * rows + 16 * i
            rest_scr[start : start + 16, :rest] = group[:, j * rest : (j + 1) * rest]
    whole = w_ref[:, :rows, :].reshape(width, main)
    half = steps // 2 * ROWS
    sides = []
    for start in (0, half):
        part = basis_scr[start : start + half, :]
        side = dot(part, whole)
        if rest:
            side = jnp.concatenate([side, dot(part, rest_scr[:, :rest])], axis=1)
        sides.append(side)
    for t in range(steps):
        start = t * ROWS % half
        a_t = sides[t * ROWS // half][start : start + ROWS]
        k = jnp.concatenate([a_t[:chans, 2 * cols :].astype(BF)] * per, axis=0)
        k = jnp.where(same, k, jnp.zeros_like(k))
        product = dot(a_t[:, :cols].astype(BF), k, ((1,), (1,)))
        if sub == chans:
            product = jnp.concatenate([product, product], axis=1)
            block = jnp.where(values, a_t[:, : 2 * cols], product)
        else:
            block = jnp.concatenate([product, a_t[:, cols : 2 * cols]], axis=1)
        before = opening_ref if t == 0 else states_ref.at[t - 1]
        groups = [before[i : i + 8, :] for i in range(0, tokd, 8)]
        last = jnp.concatenate(groups, axis=1)
        low = block[ROWS - 16 : ROWS - 8]
        if last.shape[1] > body:
            low = jnp.concatenate([low, jnp.zeros((8, last.shape[1] - body), F32)], axis=1)
        out_ref[t, : ROWS - 16, :body] = block[: ROWS - 16].astype(BF)
        out_ref[t, ROWS - 16 :, :] = jnp.concatenate([low, last], axis=0).astype(BF)


def prepare(embed, mod_all, w_mine, states, opening, per, sub):
    steps, tokd, chans = states.shape
    lanes = max(per * (chans + sub), tokd // 8 * chans)
    return pl.pallas_call(
        functools.partial(prepare_kernel, per, sub),
        out_shape=jax.ShapeDtypeStruct((steps, ROWS, lanes), BF),
        scratch_shapes=[
            pltpu.VMEM((steps * ROWS, embed.shape[1]), BF),
            pltpu.VMEM((embed.shape[1], 128), BF),
        ],
        compiler_params=params(10),
        name="prepare",
    )(embed, mod_all, w_mine, states, opening)


def attend_kernel(
    heads, n_sub, per, sub, tokd, part_ref, embed_ref, pay_ref, out_ref, queries_ref, keys_scr
):
    chans = embed_ref.shape[0]
    hdim = n_sub * sub
    length = queries_ref.shape[0]
    for source in range(pay_ref.shape[0]):
        last = pay_ref[source, ROWS - 16 :, :].astype(F32)[8:]
        for i in range(tokd // 8):
            start = source * tokd + i * 8
            keys_scr[start : start + 8, :] = last[:, i * chans : (i + 1) * chans]
    first = pl.multiple_of(part_ref[0] * length, length)

    def augmented(p):
        residual = dot(p.astype(BF), embed_ref[...])
        residual = residual - jnp.mean(residual, axis=1, keepdims=True)
        variance = jnp.mean(residual * residual, axis=1, keepdims=True)
        lane = lax.broadcasted_iota(jnp.int32, p.shape, 1)
        return jnp.concatenate([p * lax.rsqrt(variance + 1e-6), (lane == 0).astype(F32)], axis=1)

    every = augmented(keys_scr[...])
    queries = keys_scr[pl.ds(first, length), :]
    queries_ref[...] = queries.astype(BF)
    mine = every if length == keys_scr.shape[0] else augmented(queries)
    keys = every[:, :chans].astype(BF)
    every_t = every.T[: chans + 16].astype(BF)
    products, values = [], []
    for h in range(heads):
        product = None
        value_parts = []
        for j in range(n_sub):
            source, slot = divmod(h * n_sub + j, per)
            part = pay_ref[source, :, slot * chans : (slot + 1) * chans].astype(F32)
            product = part if product is None else product + part
            start = per * chans + slot * sub
            value_parts.append(pay_ref[source, :, start : start + sub])
        products.append(product.astype(BF))
        values.append(jnp.concatenate(value_parts, axis=1) if n_sub > 1 else value_parts[0])
    factor = hdim**-0.5 * math.log2(math.e)
    sides = (dot(mine[:, :ROWS].astype(BF), jnp.concatenate(products, axis=1)) * factor).astype(BF)

    def scores(h):
        return dot(keys, sides[:, h * chans : (h + 1) * chans], ((1,), (1,)))

    mixed = []
    now = scores(0)
    for h in range(heads):
        following = scores(h + 1) if h + 1 < heads else None
        weights = jnp.exp2(now - jnp.max(now, axis=0, keepdims=True)).astype(BF)
        rows = dot(every_t, weights)
        mixed.append(rows * (1.0 / rows[chans : chans + 1]))
        now = following
    for h in range(heads):
        result = dot(mixed[h].T.astype(BF), values[h])
        out_ref[:, h * hdim : (h + 1) * hdim] = result.astype(BF)


def attend(part, embed, payload, tokd, share, heads, n_sub, per, sub):
    length = payload.shape[0] * tokd
    return pl.pallas_call(
        functools.partial(attend_kernel, heads, n_sub, per, sub, tokd),
        out_shape=[
            jax.ShapeDtypeStruct((length // share, heads * n_sub * sub), BF),
            jax.ShapeDtypeStruct((length // share, embed.shape[0]), BF),
        ],
        in_specs=[SMEM, VMEM, VMEM],
        scratch_shapes=[pltpu.VMEM((length, embed.shape[0]), F32)],
        compiler_params=params(9 if share == 1 else 40),
        name="attend",
    )(part, embed, payload)


def finish_kernel(
    tokd, owner_ref, coef_ref, embed_ref, queries_ref, att_ref, gate_ref, final_ref, *refs
):
    *wo_refs, out_ref, wo_scr, sum_scr, sem = refs
    width = wo_scr.shape[1]
    chunk = width // 2
    copies = []
    for c in range(2):
        lanes = pl.ds(c * chunk, chunk)
        for i, ref in enumerate(wo_refs):
            rows = ref.shape[0]
            start = pl.multiple_of(owner_ref[i] * rows, rows)
            target = wo_scr.at[pl.ds(start, rows), lanes]
            copies.append(pltpu.make_async_copy(ref.at[:, lanes], target, sem.at[c, i]))
            copies[-1].start()
    total = 0.0
    for c in range(2):
        lanes = slice(c * chunk, (c + 1) * chunk)
        residual = dot(queries_ref[...], embed_ref[:, lanes])
        for copy in copies[c * len(wo_refs) : (c + 1) * len(wo_refs)]:
            copy.wait()
        updated = residual + gate_ref[:, lanes] * dot(att_ref[...], wo_scr[:, lanes])
        sum_scr[:, lanes] = updated
        total = total + jnp.sum(updated, axis=1, keepdims=True)
    centred = sum_scr[...] - total * (1.0 / width)
    variance = jnp.mean(centred * centred, axis=1, keepdims=True)
    normed = centred * lax.rsqrt(variance + 1e-6)
    high = normed.astype(BF)
    noise = dot(high, final_ref[...], ((1,), (1,)))
    noise = noise * coef_ref[0]
    half = tokd // 2
    for i in range(out_ref.shape[1]):
        block = noise[i * tokd : (i + 1) * tokd]
        block = jnp.concatenate([block[:half], block[half:]], axis=1).astype(BF)
        for j in range(out_ref.shape[0]):
            out_ref[j, i] = block


def finish(owners, coef, embed, queries, att, gate, final, parts, tokd, repeats):
    chans, width = final.shape
    length = queries.shape[0]
    return pl.pallas_call(
        functools.partial(finish_kernel, tokd),
        out_shape=jax.ShapeDtypeStruct((repeats, length // tokd, tokd // 2, 2 * chans), BF),
        in_specs=[SMEM] * 2 + [VMEM] * 5 + [pl.BlockSpec(memory_space=pl.ANY)] * len(parts),
        scratch_shapes=[
            pltpu.VMEM((att.shape[1], width), BF),
            pltpu.VMEM((length, width), F32),
            pltpu.SemaphoreType.DMA((2, len(parts))),
        ],
        compiler_params=params(15),
        name="finish",
    )(owners, coef, embed, queries, att, gate, final, *parts)


def advance_kernel(share, place_ref, keep_ref, noise_ref, states_ref, opening_ref, first_ref, kept_ref, out_ref, square_ref):
    groups, count = noise_ref.shape[:2]
    steps, tokd, chans = states_ref.shape
    packed = jnp.zeros(noise_ref.shape[2:], F32)
    for group in range(groups - 1):
        total = noise_ref[group, 0].astype(F32)
        for i in range(1, count):
            total = total + noise_ref[group, i].astype(F32)
        packed = packed + jnp.where(place_ref[0] > group, total, jnp.zeros_like(total))

    def unpack(x):
        return jnp.concatenate([x[:, :chans], x[:, chans:]], axis=0)

    state = first_ref[...] + kept_ref[...] + unpack(packed)
    for t in range(steps):
        noise = noise_ref[place_ref[0], t * share].astype(F32)
        for i in range(1, share):
            noise = noise + noise_ref[place_ref[0], t * share + i].astype(F32)
        before = opening_ref[...] if t == 0 else states_ref[t - 1]
        state = state + (keep_ref[t] * before + unpack(noise))
        out_ref[t] = state
        error = state - states_ref[t]
        square_ref[t : t + 1, :] = jnp.sum(error * error, axis=0, keepdims=True)


def advance(place, keep, noise, states, opening, first, kept, share):
    steps, _, chans = states.shape
    return pl.pallas_call(
        functools.partial(advance_kernel, share),
        out_shape=[
            jax.ShapeDtypeStruct(states.shape, F32),
            jax.ShapeDtypeStruct((steps, chans), F32),
        ],
        in_specs=[SMEM] * 2 + [VMEM] * 5,
        compiler_params=params(4),
        name="advance",
    )(place, keep, noise, states, opening, first, kept)


def swap(x, mask, count):
    return lax.ppermute(x, "seq", [(i, i ^ mask) for i in range(count)])


def turn_by_plane(x, count, tm_count, swapped=0):
    pairs = []
    for i in range(tm_count):
        for j in range(count):
            pairs.append((i * count + j, i * count + (j ^ (4 if (i + j + swapped) % 2 else 2))))
    return lax.ppermute(x, ("tm", "seq"), pairs)


def earlier_total(total, count):
    place = lax.axis_index("tm")
    carried = jnp.zeros_like(total)
    for by in range(1, count):
        carried += lax.ppermute(total, "tm", [(i, i + by) for i in range(count - by)])
    return carried


def total_over_seq(part, count):
    if count != 8:
        return lax.psum(part, "seq")
    part = part + swap(part, 1, count)
    return part + swap(part, 2, count) + swap(part, 4, count) + swap(part, 6, count)


def per_device(
    states,
    first_state,
    now_step,
    next_step,
    embed_weight,
    mod_weight,
    qkv_weight,
    out_weight,
    final_weight,
):
    steps, tokd, chans = states.shape
    count = lax.axis_size("seq")
    tm_count = lax.axis_size("tm")
    time_index = lax.axis_index("tm")
    seq_index = lax.axis_index("seq")
    rows, heads, width_three = qkv_weight.shape
    hdim = width_three // 3
    width = heads * hdim
    share = count // steps
    n_sub = count // math.gcd(count, heads)
    per = heads * n_sub // count
    sub = hdim // n_sub
    barrier = lax.optimization_barrier
    mine = seq_index // share
    part = seq_index % share

    w_sent = cut(jnp.transpose(qkv_weight, (1, 0, 2)), count, n_sub, per, sub)
    w_mine = lax.all_to_all(w_sent, "seq", 0, 0, tiled=True)

    by_planes = count == 8 and tm_count % 2 == 0
    if by_planes:
        first = turn_by_plane(out_weight, count, tm_count)
    late_states, _ = barrier((states, w_sent))
    edge = lax.ppermute(late_states[-1], "tm", [(i, i + 1) for i in range(tm_count - 1)])
    opening = jnp.where(time_index == 0, first_state, edge)
    keep_coef, noise_coef = coefficients(now_step, next_step)
    kept = keep_coef[0] * opening + jnp.sum(keep_coef[1:, None, None] * states[:-1], axis=0)
    kept = earlier_total(kept, tm_count)
    mod_all = modulation(now_step, mod_weight)
    gate = lax.dynamic_slice(mod_all, (mine, 2 * width), (1, width))
    coef = lax.dynamic_slice(noise_coef, (mine,), (1,))
    if by_planes:
        late_first, _ = barrier((first, (kept, mod_all, gate, coef)))
        second = lax.ppermute(late_first, "tm", [(i, i ^ 1) for i in range(tm_count)])
    w_mine, mod_all, opening, kept, gate, coef = barrier((w_mine, mod_all, opening, kept, gate, coef))
    if by_planes:
        late_first, _ = barrier((first, w_mine))
        third = turn_by_plane(late_first, count, tm_count, 1)

    payload = prepare(embed_weight, mod_all, w_mine, states, opening, per, sub)
    sent = jnp.repeat(payload, share, axis=0)
    received = lax.all_to_all(sent, "seq", 0, 0, tiled=True)
    if by_planes:
        own, first, second, _ = barrier((out_weight, first, second, payload))
        third, _ = barrier((third, received))
        parts = []
        for block in (own, first, second, third):
            parts += [block, swap(block, 1, count)]
        one = jnp.where((seq_index + time_index) % 2 == 0, 2, 4)
        two = 6 - one
        zero = jnp.zeros_like(one)
        owners = [zero, zero + 1, one, two + 1, two, one + 1, zero + 6, zero + 7]
        owners = seq_index ^ jnp.stack(owners)
    else:
        parts = [lax.all_gather(out_weight, "seq", axis=0, tiled=True)]
        owners = jnp.zeros((1,), jnp.int32)
    part_place = jnp.full((1,), part, jnp.int32)
    att, queries = attend(part_place, embed_weight, received, tokd, share, heads, n_sub, per, sub)
    repeats = tm_count if share == 1 else 1
    noise = finish(
        owners, coef, embed_weight, queries, att, gate, final_weight.T, parts, tokd, repeats
    )

    if share > 1:
        full = jnp.zeros((share,) + noise.shape[1:], BF)
        full = lax.dynamic_update_slice(full, noise, (part, 0, 0, 0))
        noise = jnp.broadcast_to(full[None], (tm_count,) + full.shape)
    block = noise.shape[-2:]
    noise = noise.reshape((tm_count * count,) + block)
    noise = lax.all_to_all(noise, ("tm", "seq"), 0, 0, tiled=True)
    noise = noise.reshape((tm_count, count) + block)
    time_place = jnp.full((1,), time_index, jnp.int32)
    advanced, squares = advance(time_place, keep_coef, noise, states, opening, first_state, kept, share)
    errors = jnp.sum(total_over_seq(squares, count), axis=1) / (tokd * count * chans)
    return (advanced, errors)


def solution(mesh):
    in_specs = (
        P("tm", "seq", None),
        P("seq", None),
        P("tm"),
        P("tm"),
        P(),
        P(),
        P("seq", None, None),
        P("seq", None),
        P(),
    )
    out_specs = (P("tm", "seq", None), P("tm"))
    return jax.shard_map(
        per_device, mesh=mesh, in_specs=in_specs, out_specs=out_specs, check_vma=False
    )
```

```python
import functools
import math

import jax
import jax.numpy as jnp
from jax import lax
from jax.experimental import pallas as pl
from jax.experimental.pallas import tpu as pltpu
from jax.sharding import PartitionSpec as P

BF = jnp.bfloat16
F32 = jnp.float32
ROWS = 80
MIB = 1024 * 1024


def dot(a, b, dims=((1,), (0,))):
    return lax.dot_general(a, b, (dims, ((), ())), preferred_element_type=F32)


def alpha_bar(step_ids):
    fraction = (step_ids.astype(F32) / 1000.0 + 0.008) / 1.008
    return jnp.cos(fraction * (math.pi / 2)) ** 2


def coefficients(now_step, next_step):
    alpha_now = alpha_bar(now_step)
    alpha_next = alpha_bar(next_step)
    step_ratio = jnp.sqrt(alpha_next / alpha_now)
    keep_coef = step_ratio - 1.0
    noise_coef = jnp.sqrt(1.0 - alpha_next) - step_ratio * jnp.sqrt(1.0 - alpha_now)
    return (keep_coef, noise_coef)


def modulation(step_ids, mod_weight):
    half_freq = mod_weight.shape[0] // 2
    frequency = jnp.exp(-math.log(10000.0) * jnp.arange(half_freq, dtype=F32) / half_freq)
    angles = step_ids.astype(F32)[:, None] * frequency[None, :]
    time_embed = jnp.concatenate([jnp.cos(angles), jnp.sin(angles)], axis=1).astype(BF)
    return jnp.dot(time_embed, mod_weight, preferred_element_type=F32)


SMEM = pl.BlockSpec(memory_space=pltpu.SMEM)
VMEM = pl.BlockSpec(memory_space=pltpu.VMEM)


def params(mib):
    return pltpu.CompilerParams(vmem_limit_bytes=mib * MIB)


def packing(rows, lanes):
    main = lanes // 128 * 128
    rest = lanes - main
    if rest == 0:
        return (main, 0, 1, 0)
    each = main // rest
    return (main, rest, each, -(-(rows // 16) // each))


def cut_kernel(n_sub, per, sub, w_ref, out_ref, w_scr, out_scr, in_sem, out_sem):
    arriving = []
    for head in range(w_ref.shape[0]):
        arriving.append(pltpu.make_async_copy(w_ref.at[head], w_scr.at[head], in_sem.at[head]))
        arriving[-1].start()
    here = 0
    leaving = []
    for dest in range(out_ref.shape[0]):
        needed = ((dest + 1) * per - 1) // n_sub + 1
        for copy in arriving[here:needed]:
            copy.wait()
        here = max(here, needed)
        pieces = []
        for kind in (0, 2, 1):
            for i in range(per):
                head, part = divmod(dest * per + i, n_sub)
                start = kind * n_sub * sub + part * sub
                pieces.append(w_scr[head, :, start : start + sub])
        block = jnp.concatenate(pieces, axis=1)
        rows, lanes = block.shape
        main, rest, each, strips = packing(rows, lanes)
        out_scr[dest, :rows, :] = block[:, :main]
        groups = [block[i : i + 16, main:] for i in range(0, rows, 16) if rest]
        groups += [jnp.zeros((16, rest), BF)] * (strips * each - len(groups))
        for i in range(strips):
            strip = jnp.concatenate(groups[i * each : (i + 1) * each], axis=1)
            out_scr[dest, rows + 16 * i : rows + 16 * (i + 1), :] = strip
        leaving.append(pltpu.make_async_copy(out_scr.at[dest], out_ref.at[dest], out_sem.at[dest]))
        leaving[-1].start()
    for copy in leaving:
        copy.wait()


def cut(w, count, n_sub, per, sub):
    main, _, _, strips = packing(w.shape[1], 3 * per * sub)
    shape = (count, w.shape[1] + 16 * strips, main)
    return pl.pallas_call(
        functools.partial(cut_kernel, n_sub, per, sub),
        out_shape=jax.ShapeDtypeStruct(shape, BF),
        in_specs=[pl.BlockSpec(memory_space=pl.ANY)],
        out_specs=pl.BlockSpec(memory_space=pl.ANY),
        scratch_shapes=[
            pltpu.VMEM(w.shape, BF),
            pltpu.VMEM(shape, BF),
            pltpu.SemaphoreType.DMA((w.shape[0],)),
            pltpu.SemaphoreType.DMA((count,)),
        ],
        compiler_params=params(56),
        name="cut",
    )(w)


def prepare_kernel(
    per, sub, embed_ref, mod_ref, w_ref, states_ref, opening_ref, out_ref, basis_scr, rest_scr
):
    steps, tokd, chans = states_ref.shape
    width = embed_ref.shape[1]
    embed = embed_ref[...].astype(F32)
    centred = embed - jnp.mean(embed, axis=1, keepdims=True)
    pad = jnp.zeros((ROWS - chans - 8, width), F32)
    first = lax.broadcasted_iota(jnp.int32, (8, width), 0) == 0
    for t in range(steps):
        shift = mod_ref[t : t + 1, :width]
        scale = mod_ref[t : t + 1, width : 2 * width]
        tail = jnp.where(first, jnp.broadcast_to(shift, (8, width)), 0.0)
        rows = jnp.concatenate([centred * (1.0 + scale), tail, pad], axis=0)
        basis_scr[t * ROWS : (t + 1) * ROWS, :] = rows.astype(BF)
    cols = per * sub
    row = lax.broadcasted_iota(jnp.int32, (per * chans, cols), 0) // chans
    lane = lax.broadcasted_iota(jnp.int32, (per * chans, cols), 1) // sub
    same = row == lane
    body = per * (chans + sub)
    values = lax.broadcasted_iota(jnp.int32, (ROWS, body), 1) >= per * chans
    rows = width // w_ref.shape[0]
    main, rest, each, _ = packing(rows, 3 * cols)
    for source in range(w_ref.shape[0]):
        for i in range(rows // 16 if rest else 0):
            strip, j = divmod(i, each)
            group = w_ref[source, rows + 16 * strip : rows + 16 * (strip + 1), :]
            start = source * rows + 16 * i
            rest_scr[start : start + 16, :rest] = group[:, j * rest : (j + 1) * rest]
    whole = w_ref[:, :rows, :].reshape(width, main)
    half = steps // 2 * ROWS
    sides = []
    for start in (0, half):
        part = basis_scr[start : start + half, :]
        side = dot(part, whole)
        if rest:
            side = jnp.concatenate([side, dot(part, rest_scr[:, :rest])], axis=1)
        sides.append(side)
    for t in range(steps):
        start = t * ROWS % half
        a_t = sides[t * ROWS // half][start : start + ROWS]
        k = jnp.concatenate([a_t[:chans, 2 * cols :].astype(BF)] * per, axis=0)
        k = jnp.where(same, k, jnp.zeros_like(k))
        product = dot(a_t[:, :cols].astype(BF), k, ((1,), (1,)))
        if sub == chans:
            product = jnp.concatenate([product, product], axis=1)
            block = jnp.where(values, a_t[:, : 2 * cols], product)
        else:
            block = jnp.concatenate([product, a_t[:, cols : 2 * cols]], axis=1)
        before = opening_ref if t == 0 else states_ref.at[t - 1]
        groups = [before[i : i + 8, :] for i in range(0, tokd, 8)]
        last = jnp.concatenate(groups, axis=1)
        low = block[ROWS - 16 : ROWS - 8]
        if last.shape[1] > body:
            low = jnp.concatenate([low, jnp.zeros((8, last.shape[1] - body), F32)], axis=1)
        out_ref[t, : ROWS - 16, :body] = block[: ROWS - 16].astype(BF)
        out_ref[t, ROWS - 16 :, :] = jnp.concatenate([low, last], axis=0).astype(BF)


def prepare(embed, mod_all, w_mine, states, opening, per, sub):
    steps, tokd, chans = states.shape
    lanes = max(per * (chans + sub), tokd // 8 * chans)
    return pl.pallas_call(
        functools.partial(prepare_kernel, per, sub),
        out_shape=jax.ShapeDtypeStruct((steps, ROWS, lanes), BF),
        scratch_shapes=[
            pltpu.VMEM((steps * ROWS, embed.shape[1]), BF),
            pltpu.VMEM((embed.shape[1], 128), BF),
        ],
        compiler_params=params(7),
        name="prepare",
    )(embed, mod_all, w_mine, states, opening)


def attend_kernel(
    heads, n_sub, per, sub, tokd, part_ref, embed_ref, pay_ref, out_ref, queries_ref, keys_scr
):
    chans = embed_ref.shape[0]
    hdim = n_sub * sub
    length = queries_ref.shape[0]
    for source in range(pay_ref.shape[0]):
        last = pay_ref[source, ROWS - 16 :, :].astype(F32)[8:]
        for i in range(tokd // 8):
            start = source * tokd + i * 8
            keys_scr[start : start + 8, :] = last[:, i * chans : (i + 1) * chans]
    first = pl.multiple_of(part_ref[0] * length, length)

    def augmented(p):
        residual = dot(p.astype(BF), embed_ref[...])
        residual = residual - jnp.mean(residual, axis=1, keepdims=True)
        variance = jnp.mean(residual * residual, axis=1, keepdims=True)
        lane = lax.broadcasted_iota(jnp.int32, p.shape, 1)
        return jnp.concatenate([p * lax.rsqrt(variance + 1e-6), (lane == 0).astype(F32)], axis=1)

    every = augmented(keys_scr[...])
    queries = keys_scr[pl.ds(first, length), :]
    queries_ref[...] = queries.astype(BF)
    mine = every if length == keys_scr.shape[0] else augmented(queries)
    keys = every[:, :chans].astype(BF)
    every_t = every.T[: chans + 16].astype(BF)
    products, values = [], []
    for h in range(heads):
        product = None
        value_parts = []
        for j in range(n_sub):
            source, slot = divmod(h * n_sub + j, per)
            part = pay_ref[source, :, slot * chans : (slot + 1) * chans].astype(F32)
            product = part if product is None else product + part
            start = per * chans + slot * sub
            value_parts.append(pay_ref[source, :, start : start + sub])
        products.append(product.astype(BF))
        values.append(jnp.concatenate(value_parts, axis=1) if n_sub > 1 else value_parts[0])
    factor = hdim**-0.5 * math.log2(math.e)
    sides = (dot(mine[:, :ROWS].astype(BF), jnp.concatenate(products, axis=1)) * factor).astype(BF)

    def scores(h):
        return dot(keys, sides[:, h * chans : (h + 1) * chans], ((1,), (1,)))

    mixed = []
    now = scores(0)
    for h in range(heads):
        following = scores(h + 1) if h + 1 < heads else None
        weights = jnp.exp2(now - jnp.max(now, axis=0, keepdims=True)).astype(BF)
        rows = dot(every_t, weights)
        mixed.append(rows * (1.0 / rows[chans : chans + 1]))
        now = following
    for h in range(heads):
        result = dot(mixed[h].T.astype(BF), values[h])
        out_ref[:, h * hdim : (h + 1) * hdim] = result.astype(BF)


def attend(part, embed, payload, tokd, share, heads, n_sub, per, sub):
    length = payload.shape[0] * tokd
    return pl.pallas_call(
        functools.partial(attend_kernel, heads, n_sub, per, sub, tokd),
        out_shape=[
            jax.ShapeDtypeStruct((length // share, heads * n_sub * sub), BF),
            jax.ShapeDtypeStruct((length // share, embed.shape[0]), BF),
        ],
        in_specs=[SMEM, VMEM, VMEM],
        scratch_shapes=[pltpu.VMEM((length, embed.shape[0]), F32)],
        compiler_params=params(7 if share == 1 else 40),
        name="attend",
    )(part, embed, payload)


def finish_kernel(
    tokd, owner_ref, coef_ref, embed_ref, queries_ref, att_ref, gate_ref, final_ref, *refs
):
    *wo_refs, out_ref, wo_scr, sum_scr, sem = refs
    width = wo_scr.shape[1]
    chunk = width // 2
    copies = []
    for c in range(2):
        lanes = pl.ds(c * chunk, chunk)
        for i, ref in enumerate(wo_refs):
            rows = ref.shape[0]
            start = pl.multiple_of(owner_ref[i] * rows, rows)
            target = wo_scr.at[pl.ds(start, rows), lanes]
            copies.append(pltpu.make_async_copy(ref.at[:, lanes], target, sem.at[c, i]))
            copies[-1].start()
    total = 0.0
    for c in range(2):
        lanes = slice(c * chunk, (c + 1) * chunk)
        residual = dot(queries_ref[...], embed_ref[:, lanes])
        for copy in copies[c * len(wo_refs) : (c + 1) * len(wo_refs)]:
            copy.wait()
        updated = residual + gate_ref[:, lanes] * dot(att_ref[...], wo_scr[:, lanes])
        sum_scr[:, lanes] = updated
        total = total + jnp.sum(updated, axis=1, keepdims=True)
    centred = sum_scr[...] - total * (1.0 / width)
    variance = jnp.mean(centred * centred, axis=1, keepdims=True)
    normed = centred * lax.rsqrt(variance + 1e-6)
    high = normed.astype(BF)
    noise = dot(high, final_ref[...], ((1,), (1,)))
    noise = noise * coef_ref[0]
    half = tokd // 2
    for i in range(out_ref.shape[1]):
        block = noise[i * tokd : (i + 1) * tokd]
        block = jnp.concatenate([block[:half], block[half:]], axis=1).astype(BF)
        for j in range(out_ref.shape[0]):
            out_ref[j, i] = block


def finish(owners, coef, embed, queries, att, gate, final, parts, tokd, repeats):
    chans, width = final.shape
    length = queries.shape[0]
    return pl.pallas_call(
        functools.partial(finish_kernel, tokd),
        out_shape=jax.ShapeDtypeStruct((repeats, length // tokd, tokd // 2, 2 * chans), BF),
        in_specs=[SMEM] * 2 + [VMEM] * 5 + [pl.BlockSpec(memory_space=pl.ANY)] * len(parts),
        scratch_shapes=[
            pltpu.VMEM((att.shape[1], width), BF),
            pltpu.VMEM((length, width), F32),
            pltpu.SemaphoreType.DMA((2, len(parts))),
        ],
        compiler_params=params(12),
        name="finish",
    )(owners, coef, embed, queries, att, gate, final, *parts)


def advance_kernel(share, place_ref, keep_ref, noise_ref, states_ref, opening_ref, first_ref, kept_ref, out_ref, square_ref):
    groups, count = noise_ref.shape[:2]
    steps, tokd, chans = states_ref.shape
    packed = jnp.zeros(noise_ref.shape[2:], F32)
    for group in range(groups - 1):
        total = noise_ref[group, 0].astype(F32)
        for i in range(1, count):
            total = total + noise_ref[group, i].astype(F32)
        packed = packed + jnp.where(place_ref[0] > group, total, jnp.zeros_like(total))

    def unpack(x):
        return jnp.concatenate([x[:, :chans], x[:, chans:]], axis=0)

    state = first_ref[...] + kept_ref[...] + unpack(packed)
    for t in range(steps):
        noise = noise_ref[place_ref[0], t * share].astype(F32)
        for i in range(1, share):
            noise = noise + noise_ref[place_ref[0], t * share + i].astype(F32)
        before = opening_ref[...] if t == 0 else states_ref[t - 1]
        state = state + (keep_ref[t] * before + unpack(noise))
        out_ref[t] = state
        error = state - states_ref[t]
        square_ref[t : t + 1, :] = jnp.sum(error * error, axis=0, keepdims=True)


def advance(place, keep, noise, states, opening, first, kept, share):
    steps, _, chans = states.shape
    return pl.pallas_call(
        functools.partial(advance_kernel, share),
        out_shape=[
            jax.ShapeDtypeStruct(states.shape, F32),
            jax.ShapeDtypeStruct((steps, chans), F32),
        ],
        in_specs=[SMEM] * 2 + [VMEM] * 5,
        compiler_params=params(2),
        name="advance",
    )(place, keep, noise, states, opening, first, kept)


def swap(x, mask, count):
    return lax.ppermute(x, "seq", [(i, i ^ mask) for i in range(count)])


def turn_by_plane(x, count, tm_count, swapped=0):
    pairs = []
    for i in range(tm_count):
        for j in range(count):
            pairs.append((i * count + j, i * count + (j ^ (4 if (i + j + swapped) % 2 else 2))))
    return lax.ppermute(x, ("tm", "seq"), pairs)


def earlier_total(total, count):
    place = lax.axis_index("tm")
    carried = jnp.zeros_like(total)
    for by in range(1, count):
        carried += lax.ppermute(total, "tm", [(i, i + by) for i in range(count - by)])
    return carried


def total_over_seq(part, count):
    if count != 8:
        return lax.psum(part, "seq")
    part = part + swap(part, 1, count)
    return part + swap(part, 2, count) + swap(part, 4, count) + swap(part, 6, count)


def per_device(
    states,
    first_state,
    now_step,
    next_step,
    embed_weight,
    mod_weight,
    qkv_weight,
    out_weight,
    final_weight,
):
    steps, tokd, chans = states.shape
    count = lax.axis_size("seq")
    tm_count = lax.axis_size("tm")
    time_index = lax.axis_index("tm")
    seq_index = lax.axis_index("seq")
    rows, heads, width_three = qkv_weight.shape
    hdim = width_three // 3
    width = heads * hdim
    share = count // steps
    n_sub = count // math.gcd(count, heads)
    per = heads * n_sub // count
    sub = hdim // n_sub
    barrier = lax.optimization_barrier
    mine = seq_index // share
    part = seq_index % share

    w_sent = cut(jnp.transpose(qkv_weight, (1, 0, 2)), count, n_sub, per, sub)
    w_mine = lax.all_to_all(w_sent, "seq", 0, 0, tiled=True)

    by_planes = count == 8 and tm_count % 2 == 0
    if by_planes:
        first = turn_by_plane(out_weight, count, tm_count)
    late_states, _ = barrier((states, w_sent))
    edge = lax.ppermute(late_states[-1], "tm", [(i, i + 1) for i in range(tm_count - 1)])
    opening = jnp.where(time_index == 0, first_state, edge)
    keep_coef, noise_coef = coefficients(now_step, next_step)
    kept = keep_coef[0] * opening + jnp.sum(keep_coef[1:, None, None] * states[:-1], axis=0)
    kept = earlier_total(kept, tm_count)
    mod_all = modulation(now_step, mod_weight)
    gate = lax.dynamic_slice(mod_all, (mine, 2 * width), (1, width))
    coef = lax.dynamic_slice(noise_coef, (mine,), (1,))
    if by_planes:
        late_first, _ = barrier((first, opening))
        second = lax.ppermute(late_first, "tm", [(i, i ^ 1) for i in range(tm_count)])
    w_mine, mod_all, opening, kept, gate, coef = barrier((w_mine, mod_all, opening, kept, gate, coef))
    if by_planes:
        late_first, _ = barrier((first, w_mine))
        third = turn_by_plane(late_first, count, tm_count, 1)

    payload = prepare(embed_weight, mod_all, w_mine, states, opening, per, sub)
    sent = jnp.repeat(payload, share, axis=0)
    received = lax.all_to_all(sent, "seq", 0, 0, tiled=True)
    if by_planes:
        own, first, second, _ = barrier((out_weight, first, second, payload))
        third, _ = barrier((third, received))
        parts = []
        for block in (own, first, second, third):
            parts += [block, swap(block, 1, count)]
        one = jnp.where((seq_index + time_index) % 2 == 0, 2, 4)
        two = 6 - one
        zero = jnp.zeros_like(one)
        owners = [zero, zero + 1, one, two + 1, two, one + 1, zero + 6, zero + 7]
        owners = seq_index ^ jnp.stack(owners)
    else:
        parts = [lax.all_gather(out_weight, "seq", axis=0, tiled=True)]
        owners = jnp.zeros((1,), jnp.int32)
    part_place = jnp.full((1,), part, jnp.int32)
    att, queries = attend(part_place, embed_weight, received, tokd, share, heads, n_sub, per, sub)
    repeats = tm_count if share == 1 else 1
    noise = finish(
        owners, coef, embed_weight, queries, att, gate, final_weight.T, parts, tokd, repeats
    )

    if share > 1:
        full = jnp.zeros((share,) + noise.shape[1:], BF)
        full = lax.dynamic_update_slice(full, noise, (part, 0, 0, 0))
        noise = jnp.broadcast_to(full[None], (tm_count,) + full.shape)
    block = noise.shape[-2:]
    noise = noise.reshape((tm_count * count,) + block)
    noise = lax.all_to_all(noise, ("tm", "seq"), 0, 0, tiled=True)
    noise = noise.reshape((tm_count, count) + block)
    time_place = jnp.full((1,), time_index, jnp.int32)
    advanced, squares = advance(time_place, keep_coef, noise, states, opening, first_state, kept, share)
    errors = jnp.sum(total_over_seq(squares, count), axis=1) / (tokd * count * chans)
    return (advanced, errors)


def solution(mesh):
    in_specs = (
        P("tm", "seq", None),
        P("seq", None),
        P("tm"),
        P("tm"),
        P(),
        P(),
        P("seq", None, None),
        P("seq", None),
        P(),
    )
    out_specs = (P("tm", "seq", None), P("tm"))
    return jax.shard_map(
        per_device, mesh=mesh, in_specs=in_specs, out_specs=out_specs, check_vma=False
    )
```

```python
import functools
import math

import jax
import jax.numpy as jnp
from jax import lax
from jax.experimental import pallas as pl
from jax.experimental.pallas import tpu as pltpu
from jax.sharding import PartitionSpec as P

BF = jnp.bfloat16
F32 = jnp.float32
ROWS = 80
MIB = 1024 * 1024


def dot(a, b, dims=((1,), (0,))):
    return lax.dot_general(a, b, (dims, ((), ())), preferred_element_type=F32)


def alpha_bar(step_ids):
    fraction = (step_ids.astype(F32) / 1000.0 + 0.008) / 1.008
    return jnp.cos(fraction * (math.pi / 2)) ** 2


def coefficients(now_step, next_step):
    alpha_now = alpha_bar(now_step)
    alpha_next = alpha_bar(next_step)
    step_ratio = jnp.sqrt(alpha_next / alpha_now)
    keep_coef = step_ratio - 1.0
    noise_coef = jnp.sqrt(1.0 - alpha_next) - step_ratio * jnp.sqrt(1.0 - alpha_now)
    return (keep_coef, noise_coef)


def modulation(step_ids, mod_weight):
    half_freq = mod_weight.shape[0] // 2
    frequency = jnp.exp(-math.log(10000.0) * jnp.arange(half_freq, dtype=F32) / half_freq)
    angles = step_ids.astype(F32)[:, None] * frequency[None, :]
    time_embed = jnp.concatenate([jnp.cos(angles), jnp.sin(angles)], axis=1).astype(BF)
    return jnp.dot(time_embed, mod_weight, preferred_element_type=F32)


SMEM = pl.BlockSpec(memory_space=pltpu.SMEM)
VMEM = pl.BlockSpec(memory_space=pltpu.VMEM)


def params(mib):
    return pltpu.CompilerParams(vmem_limit_bytes=mib * MIB)


def packing(rows, lanes):
    main = lanes // 128 * 128
    rest = lanes - main
    if rest == 0:
        return (main, 0, 1, 0)
    each = main // rest
    return (main, rest, each, -(-(rows // 16) // each))


def cut_kernel(n_sub, per, sub, w_ref, out_ref, w_scr, out_scr, in_sem, out_sem):
    arriving = []
    for head in range(w_ref.shape[0]):
        arriving.append(pltpu.make_async_copy(w_ref.at[head], w_scr.at[head], in_sem.at[head]))
        arriving[-1].start()
    here = 0
    leaving = []
    for dest in range(out_ref.shape[0]):
        needed = ((dest + 1) * per - 1) // n_sub + 1
        for copy in arriving[here:needed]:
            copy.wait()
        here = max(here, needed)
        pieces = []
        for kind in (0, 2, 1):
            for i in range(per):
                head, part = divmod(dest * per + i, n_sub)
                start = kind * n_sub * sub + part * sub
                pieces.append(w_scr[head, :, start : start + sub])
        block = jnp.concatenate(pieces, axis=1)
        rows, lanes = block.shape
        main, rest, each, strips = packing(rows, lanes)
        out_scr[dest, :rows, :] = block[:, :main]
        groups = [block[i : i + 16, main:] for i in range(0, rows, 16) if rest]
        groups += [jnp.zeros((16, rest), BF)] * (strips * each - len(groups))
        for i in range(strips):
            strip = jnp.concatenate(groups[i * each : (i + 1) * each], axis=1)
            out_scr[dest, rows + 16 * i : rows + 16 * (i + 1), :] = strip
        leaving.append(pltpu.make_async_copy(out_scr.at[dest], out_ref.at[dest], out_sem.at[dest]))
        leaving[-1].start()
    for copy in leaving:
        copy.wait()


def cut(w, count, n_sub, per, sub):
    main, _, _, strips = packing(w.shape[1], 3 * per * sub)
    shape = (count, w.shape[1] + 16 * strips, main)
    return pl.pallas_call(
        functools.partial(cut_kernel, n_sub, per, sub),
        out_shape=jax.ShapeDtypeStruct(shape, BF),
        in_specs=[pl.BlockSpec(memory_space=pl.ANY)],
        out_specs=pl.BlockSpec(memory_space=pl.ANY),
        scratch_shapes=[
            pltpu.VMEM(w.shape, BF),
            pltpu.VMEM(shape, BF),
            pltpu.SemaphoreType.DMA((w.shape[0],)),
            pltpu.SemaphoreType.DMA((count,)),
        ],
        compiler_params=params(62),
        name="cut",
    )(w)


def prepare_kernel(
    per, sub, embed_ref, mod_ref, w_ref, states_ref, opening_ref, out_ref, basis_scr, rest_scr
):
    steps, tokd, chans = states_ref.shape
    width = embed_ref.shape[1]
    embed = embed_ref[...].astype(F32)
    centred = embed - jnp.mean(embed, axis=1, keepdims=True)
    pad = jnp.zeros((ROWS - chans - 8, width), F32)
    first = lax.broadcasted_iota(jnp.int32, (8, width), 0) == 0
    for t in range(steps):
        shift = mod_ref[t : t + 1, :width]
        scale = mod_ref[t : t + 1, width : 2 * width]
        tail = jnp.where(first, jnp.broadcast_to(shift, (8, width)), 0.0)
        rows = jnp.concatenate([centred * (1.0 + scale), tail, pad], axis=0)
        basis_scr[t * ROWS : (t + 1) * ROWS, :] = rows.astype(BF)
    cols = per * sub
    row = lax.broadcasted_iota(jnp.int32, (per * chans, cols), 0) // chans
    lane = lax.broadcasted_iota(jnp.int32, (per * chans, cols), 1) // sub
    same = row == lane
    body = per * (chans + sub)
    values = lax.broadcasted_iota(jnp.int32, (ROWS, body), 1) >= per * chans
    rows = width // w_ref.shape[0]
    main, rest, each, _ = packing(rows, 3 * cols)
    for source in range(w_ref.shape[0]):
        for i in range(rows // 16 if rest else 0):
            strip, j = divmod(i, each)
            group = w_ref[source, rows + 16 * strip : rows + 16 * (strip + 1), :]
            start = source * rows + 16 * i
            rest_scr[start : start + 16, :rest] = group[:, j * rest : (j + 1) * rest]
    whole = w_ref[:, :rows, :].reshape(width, main)
    half = steps // 2 * ROWS
    sides = []
    for start in (0, half):
        part = basis_scr[start : start + half, :]
        side = dot(part, whole)
        if rest:
            side = jnp.concatenate([side, dot(part, rest_scr[:, :rest])], axis=1)
        sides.append(side)
    for t in range(steps):
        start = t * ROWS % half
        a_t = sides[t * ROWS // half][start : start + ROWS]
        k = jnp.concatenate([a_t[:chans, 2 * cols :].astype(BF)] * per, axis=0)
        k = jnp.where(same, k, jnp.zeros_like(k))
        product = dot(a_t[:, :cols].astype(BF), k, ((1,), (1,)))
        if sub == chans:
            product = jnp.concatenate([product, product], axis=1)
            block = jnp.where(values, a_t[:, : 2 * cols], product)
        else:
            block = jnp.concatenate([product, a_t[:, cols : 2 * cols]], axis=1)
        before = opening_ref if t == 0 else states_ref.at[t - 1]
        groups = [before[i : i + 8, :] for i in range(0, tokd, 8)]
        last = jnp.concatenate(groups, axis=1)
        low = block[ROWS - 16 : ROWS - 8]
        if last.shape[1] > body:
            low = jnp.concatenate([low, jnp.zeros((8, last.shape[1] - body), F32)], axis=1)
        out_ref[t, : ROWS - 16, :body] = block[: ROWS - 16].astype(BF)
        out_ref[t, ROWS - 16 :, :] = jnp.concatenate([low, last], axis=0).astype(BF)


def prepare(embed, mod_all, w_mine, states, opening, per, sub):
    steps, tokd, chans = states.shape
    lanes = max(per * (chans + sub), tokd // 8 * chans)
    return pl.pallas_call(
        functools.partial(prepare_kernel, per, sub),
        out_shape=jax.ShapeDtypeStruct((steps, ROWS, lanes), BF),
        scratch_shapes=[
            pltpu.VMEM((steps * ROWS, embed.shape[1]), BF),
            pltpu.VMEM((embed.shape[1], 128), BF),
        ],
        compiler_params=params(7),
        name="prepare",
    )(embed, mod_all, w_mine, states, opening)


def attend_kernel(
    heads, n_sub, per, sub, tokd, part_ref, embed_ref, pay_ref, out_ref, queries_ref, keys_scr
):
    chans = embed_ref.shape[0]
    hdim = n_sub * sub
    length = queries_ref.shape[0]
    for source in range(pay_ref.shape[0]):
        last = pay_ref[source, ROWS - 16 :, :].astype(F32)[8:]
        for i in range(tokd // 8):
            start = source * tokd + i * 8
            keys_scr[start : start + 8, :] = last[:, i * chans : (i + 1) * chans]
    first = pl.multiple_of(part_ref[0] * length, length)

    def augmented(p):
        residual = dot(p.astype(BF), embed_ref[...])
        residual = residual - jnp.mean(residual, axis=1, keepdims=True)
        variance = jnp.mean(residual * residual, axis=1, keepdims=True)
        lane = lax.broadcasted_iota(jnp.int32, p.shape, 1)
        return jnp.concatenate([p * lax.rsqrt(variance + 1e-6), (lane == 0).astype(F32)], axis=1)

    every = augmented(keys_scr[...])
    queries = keys_scr[pl.ds(first, length), :]
    queries_ref[...] = queries.astype(BF)
    mine = every if length == keys_scr.shape[0] else augmented(queries)
    keys = every[:, :chans].astype(BF)
    every_t = every.T[: chans + 16].astype(BF)
    products, values = [], []
    for h in range(heads):
        product = None
        value_parts = []
        for j in range(n_sub):
            source, slot = divmod(h * n_sub + j, per)
            part = pay_ref[source, :, slot * chans : (slot + 1) * chans].astype(F32)
            product = part if product is None else product + part
            start = per * chans + slot * sub
            value_parts.append(pay_ref[source, :, start : start + sub])
        products.append(product.astype(BF))
        values.append(jnp.concatenate(value_parts, axis=1) if n_sub > 1 else value_parts[0])
    factor = hdim**-0.5 * math.log2(math.e)
    sides = (dot(mine[:, :ROWS].astype(BF), jnp.concatenate(products, axis=1)) * factor).astype(BF)

    def scores(h):
        return dot(keys, sides[:, h * chans : (h + 1) * chans], ((1,), (1,)))

    mixed = []
    now = scores(0)
    for h in range(heads):
        following = scores(h + 1) if h + 1 < heads else None
        weights = jnp.exp2(now - jnp.max(now, axis=0, keepdims=True)).astype(BF)
        rows = dot(every_t, weights)
        mixed.append(rows * (1.0 / rows[chans : chans + 1]))
        now = following
    for h in range(heads):
        result = dot(mixed[h].T.astype(BF), values[h])
        out_ref[:, h * hdim : (h + 1) * hdim] = result.astype(BF)


def attend(part, embed, payload, tokd, share, heads, n_sub, per, sub):
    length = payload.shape[0] * tokd
    return pl.pallas_call(
        functools.partial(attend_kernel, heads, n_sub, per, sub, tokd),
        out_shape=[
            jax.ShapeDtypeStruct((length // share, heads * n_sub * sub), BF),
            jax.ShapeDtypeStruct((length // share, embed.shape[0]), BF),
        ],
        in_specs=[SMEM, VMEM, VMEM],
        scratch_shapes=[pltpu.VMEM((length, embed.shape[0]), F32)],
        compiler_params=params(7 if share == 1 else 40),
        name="attend",
    )(part, embed, payload)


def finish_kernel(
    tokd, owner_ref, coef_ref, embed_ref, queries_ref, att_ref, gate_ref, final_ref, *refs
):
    *wo_refs, out_ref, wo_scr, sum_scr, sem = refs
    width = wo_scr.shape[1]
    chunk = width // 2
    copies = []
    for c in range(2):
        lanes = pl.ds(c * chunk, chunk)
        for i, ref in enumerate(wo_refs):
            rows = ref.shape[0]
            start = pl.multiple_of(owner_ref[i] * rows, rows)
            target = wo_scr.at[pl.ds(start, rows), lanes]
            copies.append(pltpu.make_async_copy(ref.at[:, lanes], target, sem.at[c, i]))
            copies[-1].start()
    total = 0.0
    for c in range(2):
        lanes = slice(c * chunk, (c + 1) * chunk)
        residual = dot(queries_ref[...], embed_ref[:, lanes])
        for copy in copies[c * len(wo_refs) : (c + 1) * len(wo_refs)]:
            copy.wait()
        updated = residual + gate_ref[:, lanes] * dot(att_ref[...], wo_scr[:, lanes])
        sum_scr[:, lanes] = updated
        total = total + jnp.sum(updated, axis=1, keepdims=True)
    centred = sum_scr[...] - total * (1.0 / width)
    variance = jnp.mean(centred * centred, axis=1, keepdims=True)
    normed = centred * lax.rsqrt(variance + 1e-6)
    high = normed.astype(BF)
    noise = dot(high, final_ref[...], ((1,), (1,)))
    noise = noise * coef_ref[0]
    half = tokd // 2
    for i in range(out_ref.shape[1]):
        block = noise[i * tokd : (i + 1) * tokd]
        block = jnp.concatenate([block[:half], block[half:]], axis=1).astype(BF)
        for j in range(out_ref.shape[0]):
            out_ref[j, i] = block


def finish(owners, coef, embed, queries, att, gate, final, parts, tokd, repeats):
    chans, width = final.shape
    length = queries.shape[0]
    return pl.pallas_call(
        functools.partial(finish_kernel, tokd),
        out_shape=jax.ShapeDtypeStruct((repeats, length // tokd, tokd // 2, 2 * chans), BF),
        in_specs=[SMEM] * 2 + [VMEM] * 5 + [pl.BlockSpec(memory_space=pl.ANY)] * len(parts),
        scratch_shapes=[
            pltpu.VMEM((att.shape[1], width), BF),
            pltpu.VMEM((length, width), F32),
            pltpu.SemaphoreType.DMA((2, len(parts))),
        ],
        compiler_params=params(12),
        name="finish",
    )(owners, coef, embed, queries, att, gate, final, *parts)


def advance_kernel(share, place_ref, keep_ref, noise_ref, states_ref, opening_ref, first_ref, kept_ref, out_ref, square_ref):
    groups, count = noise_ref.shape[:2]
    steps, tokd, chans = states_ref.shape
    packed = jnp.zeros(noise_ref.shape[2:], F32)
    for group in range(groups - 1):
        total = noise_ref[group, 0].astype(F32)
        for i in range(1, count):
            total = total + noise_ref[group, i].astype(F32)
        packed = packed + jnp.where(place_ref[0] > group, total, jnp.zeros_like(total))

    def unpack(x):
        return jnp.concatenate([x[:, :chans], x[:, chans:]], axis=0)

    state = first_ref[...] + kept_ref[...] + unpack(packed)
    for t in range(steps):
        noise = noise_ref[place_ref[0], t * share].astype(F32)
        for i in range(1, share):
            noise = noise + noise_ref[place_ref[0], t * share + i].astype(F32)
        before = opening_ref[...] if t == 0 else states_ref[t - 1]
        state = state + (keep_ref[t] * before + unpack(noise))
        out_ref[t] = state
        error = state - states_ref[t]
        square_ref[t : t + 1, :] = jnp.sum(error * error, axis=0, keepdims=True)


def advance(place, keep, noise, states, opening, first, kept, share):
    steps, _, chans = states.shape
    return pl.pallas_call(
        functools.partial(advance_kernel, share),
        out_shape=[
            jax.ShapeDtypeStruct(states.shape, F32),
            jax.ShapeDtypeStruct((steps, chans), F32),
        ],
        in_specs=[SMEM] * 2 + [VMEM] * 5,
        compiler_params=params(2),
        name="advance",
    )(place, keep, noise, states, opening, first, kept)


def swap(x, mask, count):
    return lax.ppermute(x, "seq", [(i, i ^ mask) for i in range(count)])


def turn_by_plane(x, count, tm_count, swapped=0):
    pairs = []
    for i in range(tm_count):
        for j in range(count):
            pairs.append((i * count + j, i * count + (j ^ (4 if (i + j + swapped) % 2 else 2))))
    return lax.ppermute(x, ("tm", "seq"), pairs)


def earlier_total(total, count):
    place = lax.axis_index("tm")
    carried = jnp.zeros_like(total)
    for by in range(1, count):
        carried += lax.ppermute(total, "tm", [(i, i + by) for i in range(count - by)])
    return carried


def total_over_seq(part, count):
    if count != 8:
        return lax.psum(part, "seq")
    part = part + swap(part, 1, count)
    return part + swap(part, 2, count) + swap(part, 4, count) + swap(part, 6, count)


def per_device(
    states,
    first_state,
    now_step,
    next_step,
    embed_weight,
    mod_weight,
    qkv_weight,
    out_weight,
    final_weight,
):
    steps, tokd, chans = states.shape
    count = lax.axis_size("seq")
    tm_count = lax.axis_size("tm")
    time_index = lax.axis_index("tm")
    seq_index = lax.axis_index("seq")
    rows, heads, width_three = qkv_weight.shape
    hdim = width_three // 3
    width = heads * hdim
    share = count // steps
    n_sub = count // math.gcd(count, heads)
    per = heads * n_sub // count
    sub = hdim // n_sub
    barrier = lax.optimization_barrier
    mine = seq_index // share
    part = seq_index % share

    w_sent = cut(jnp.transpose(qkv_weight, (1, 0, 2)), count, n_sub, per, sub)
    w_mine = lax.all_to_all(w_sent, "seq", 0, 0, tiled=True)

    by_planes = count == 8 and tm_count % 2 == 0
    if by_planes:
        first = turn_by_plane(out_weight, count, tm_count)
    late_states, _ = barrier((states, w_sent))
    edge = lax.ppermute(late_states[-1], "tm", [(i, i + 1) for i in range(tm_count - 1)])
    opening = jnp.where(time_index == 0, first_state, edge)
    keep_coef, noise_coef = coefficients(now_step, next_step)
    kept = keep_coef[0] * opening + jnp.sum(keep_coef[1:, None, None] * states[:-1], axis=0)
    kept = earlier_total(kept, tm_count)
    mod_all = modulation(now_step, mod_weight)
    gate = lax.dynamic_slice(mod_all, (mine, 2 * width), (1, width))
    coef = lax.dynamic_slice(noise_coef, (mine,), (1,))
    if by_planes:
        late_first, _ = barrier((first, opening))
        second = lax.ppermute(late_first, "tm", [(i, i ^ 1) for i in range(tm_count)])
    w_mine, mod_all, opening, kept, gate, coef = barrier((w_mine, mod_all, opening, kept, gate, coef))
    if by_planes:
        late_first, _ = barrier((first, w_mine))
        third = turn_by_plane(late_first, count, tm_count, 1)

    payload = prepare(embed_weight, mod_all, w_mine, states, opening, per, sub)
    sent = jnp.repeat(payload, share, axis=0)
    received = lax.all_to_all(sent, "seq", 0, 0, tiled=True)
    if by_planes:
        own, first, second, _ = barrier((out_weight, first, second, payload))
        third, _ = barrier((third, received))
        parts = []
        for block in (own, first, second, third):
            parts += [block, swap(block, 1, count)]
        one = jnp.where((seq_index + time_index) % 2 == 0, 2, 4)
        two = 6 - one
        zero = jnp.zeros_like(one)
        owners = [zero, zero + 1, one, two + 1, two, one + 1, zero + 6, zero + 7]
        owners = seq_index ^ jnp.stack(owners)
    else:
        parts = [lax.all_gather(out_weight, "seq", axis=0, tiled=True)]
        owners = jnp.zeros((1,), jnp.int32)
    part_place = jnp.full((1,), part, jnp.int32)
    att, queries = attend(part_place, embed_weight, received, tokd, share, heads, n_sub, per, sub)
    repeats = tm_count if share == 1 else 1
    noise = finish(
        owners, coef, embed_weight, queries, att, gate, final_weight.T, parts, tokd, repeats
    )

    if share > 1:
        full = jnp.zeros((share,) + noise.shape[1:], BF)
        full = lax.dynamic_update_slice(full, noise, (part, 0, 0, 0))
        noise = jnp.broadcast_to(full[None], (tm_count,) + full.shape)
    block = noise.shape[-2:]
    noise = noise.reshape((tm_count * count,) + block)
    noise = lax.all_to_all(noise, ("tm", "seq"), 0, 0, tiled=True)
    noise = noise.reshape((tm_count, count) + block)
    time_place = jnp.full((1,), time_index, jnp.int32)
    advanced, squares = advance(time_place, keep_coef, noise, states, opening, first_state, kept, share)
    errors = jnp.sum(total_over_seq(squares, count), axis=1) / (tokd * count * chans)
    return (advanced, errors)


def solution(mesh):
    in_specs = (
        P("tm", "seq", None),
        P("seq", None),
        P("tm"),
        P("tm"),
        P(),
        P(),
        P("seq", None, None),
        P("seq", None),
        P(),
    )
    out_specs = (P("tm", "seq", None), P("tm"))
    return jax.shard_map(
        per_device, mesh=mesh, in_specs=in_specs, out_specs=out_specs, check_vma=False
    )
```

```python
import functools
import math

import jax
import jax.numpy as jnp
from jax import lax
from jax.experimental import pallas as pl
from jax.experimental.pallas import tpu as pltpu
from jax.sharding import PartitionSpec as P

BF = jnp.bfloat16
F32 = jnp.float32
ROWS = 80
MIB = 1024 * 1024


def dot(a, b, dims=((1,), (0,))):
    return lax.dot_general(a, b, (dims, ((), ())), preferred_element_type=F32)


def alpha_bar(step_ids):
    fraction = (step_ids.astype(F32) / 1000.0 + 0.008) / 1.008
    return jnp.cos(fraction * (math.pi / 2)) ** 2


def coefficients(now_step, next_step):
    alpha_now = alpha_bar(now_step)
    alpha_next = alpha_bar(next_step)
    step_ratio = jnp.sqrt(alpha_next / alpha_now)
    keep_coef = step_ratio - 1.0
    noise_coef = jnp.sqrt(1.0 - alpha_next) - step_ratio * jnp.sqrt(1.0 - alpha_now)
    return (keep_coef, noise_coef)


def modulation(step_ids, mod_weight):
    half_freq = mod_weight.shape[0] // 2
    frequency = jnp.exp(-math.log(10000.0) * jnp.arange(half_freq, dtype=F32) / half_freq)
    angles = step_ids.astype(F32)[:, None] * frequency[None, :]
    time_embed = jnp.concatenate([jnp.cos(angles), jnp.sin(angles)], axis=1).astype(BF)
    return jnp.dot(time_embed, mod_weight, preferred_element_type=F32)


SMEM = pl.BlockSpec(memory_space=pltpu.SMEM)
VMEM = pl.BlockSpec(memory_space=pltpu.VMEM)


def params(mib):
    return pltpu.CompilerParams(vmem_limit_bytes=mib * MIB)


def packing(rows, lanes):
    main = lanes // 128 * 128
    rest = lanes - main
    if rest == 0:
        return (main, 0, 1, 0)
    each = main // rest
    return (main, rest, each, -(-(rows // 16) // each))


def cut_kernel(n_sub, per, sub, w_ref, out_ref, w_scr, out_scr, in_sem, out_sem):
    arriving = []
    for head in range(w_ref.shape[0]):
        arriving.append(pltpu.make_async_copy(w_ref.at[head], w_scr.at[head], in_sem.at[head]))
        arriving[-1].start()
    here = 0
    leaving = []
    for dest in range(out_ref.shape[0]):
        needed = ((dest + 1) * per - 1) // n_sub + 1
        for copy in arriving[here:needed]:
            copy.wait()
        here = max(here, needed)
        pieces = []
        for kind in (0, 2, 1):
            for i in range(per):
                head, part = divmod(dest * per + i, n_sub)
                start = kind * n_sub * sub + part * sub
                pieces.append(w_scr[head, :, start : start + sub])
        block = jnp.concatenate(pieces, axis=1)
        rows, lanes = block.shape
        main, rest, each, strips = packing(rows, lanes)
        out_scr[dest, :rows, :] = block[:, :main]
        groups = [block[i : i + 16, main:] for i in range(0, rows, 16) if rest]
        groups += [jnp.zeros((16, rest), BF)] * (strips * each - len(groups))
        for i in range(strips):
            strip = jnp.concatenate(groups[i * each : (i + 1) * each], axis=1)
            out_scr[dest, rows + 16 * i : rows + 16 * (i + 1), :] = strip
        leaving.append(pltpu.make_async_copy(out_scr.at[dest], out_ref.at[dest], out_sem.at[dest]))
        leaving[-1].start()
    for copy in leaving:
        copy.wait()


def cut(w, count, n_sub, per, sub):
    main, _, _, strips = packing(w.shape[1], 3 * per * sub)
    shape = (count, w.shape[1] + 16 * strips, main)
    return pl.pallas_call(
        functools.partial(cut_kernel, n_sub, per, sub),
        out_shape=jax.ShapeDtypeStruct(shape, BF),
        in_specs=[pl.BlockSpec(memory_space=pl.ANY)],
        out_specs=pl.BlockSpec(memory_space=pl.ANY),
        scratch_shapes=[
            pltpu.VMEM(w.shape, BF),
            pltpu.VMEM(shape, BF),
            pltpu.SemaphoreType.DMA((w.shape[0],)),
            pltpu.SemaphoreType.DMA((count,)),
        ],
        compiler_params=params(62),
        name="cut",
    )(w)


def prepare_kernel(
    per, sub, embed_ref, mod_ref, w_ref, states_ref, opening_ref, out_ref, basis_scr, rest_scr
):
    steps, tokd, chans = states_ref.shape
    width = embed_ref.shape[1]
    embed = embed_ref[...].astype(F32)
    centred = embed - jnp.mean(embed, axis=1, keepdims=True)
    pad = jnp.zeros((ROWS - chans - 8, width), F32)
    first = lax.broadcasted_iota(jnp.int32, (8, width), 0) == 0
    for t in range(steps):
        shift = mod_ref[t : t + 1, :width]
        scale = mod_ref[t : t + 1, width : 2 * width]
        tail = jnp.where(first, jnp.broadcast_to(shift, (8, width)), 0.0)
        rows = jnp.concatenate([centred * (1.0 + scale), tail, pad], axis=0)
        basis_scr[t * ROWS : (t + 1) * ROWS, :] = rows.astype(BF)
    cols = per * sub
    row = lax.broadcasted_iota(jnp.int32, (per * chans, cols), 0) // chans
    lane = lax.broadcasted_iota(jnp.int32, (per * chans, cols), 1) // sub
    same = row == lane
    body = per * (chans + sub)
    values = lax.broadcasted_iota(jnp.int32, (ROWS, body), 1) >= per * chans
    rows = width // w_ref.shape[0]
    main, rest, each, _ = packing(rows, 3 * cols)
    for source in range(w_ref.shape[0]):
        for i in range(rows // 16 if rest else 0):
            strip, j = divmod(i, each)
            group = w_ref[source, rows + 16 * strip : rows + 16 * (strip + 1), :]
            start = source * rows + 16 * i
            rest_scr[start : start + 16, :rest] = group[:, j * rest : (j + 1) * rest]
    whole = w_ref[:, :rows, :].reshape(width, main)
    half = steps // 2 * ROWS
    sides = []
    for start in (0, half):
        part = basis_scr[start : start + half, :]
        side = dot(part, whole)
        if rest:
            side = jnp.concatenate([side, dot(part, rest_scr[:, :rest])], axis=1)
        sides.append(side)
    for t in range(steps):
        start = t * ROWS % half
        a_t = sides[t * ROWS // half][start : start + ROWS]
        k = jnp.concatenate([a_t[:chans, 2 * cols :].astype(BF)] * per, axis=0)
        k = jnp.where(same, k, jnp.zeros_like(k))
        product = dot(a_t[:, :cols].astype(BF), k, ((1,), (1,)))
        if sub == chans:
            product = jnp.concatenate([product, product], axis=1)
            block = jnp.where(values, a_t[:, : 2 * cols], product)
        else:
            block = jnp.concatenate([product, a_t[:, cols : 2 * cols]], axis=1)
        before = opening_ref if t == 0 else states_ref.at[t - 1]
        groups = [before[i : i + 8, :] for i in range(0, tokd, 8)]
        last = jnp.concatenate(groups, axis=1)
        low = block[ROWS - 16 : ROWS - 8]
        if last.shape[1] > body:
            low = jnp.concatenate([low, jnp.zeros((8, last.shape[1] - body), F32)], axis=1)
        out_ref[t, : ROWS - 16, :body] = block[: ROWS - 16].astype(BF)
        out_ref[t, ROWS - 16 :, :] = jnp.concatenate([low, last], axis=0).astype(BF)


def prepare(embed, mod_all, w_mine, states, opening, per, sub):
    steps, tokd, chans = states.shape
    lanes = max(per * (chans + sub), tokd // 8 * chans)
    return pl.pallas_call(
        functools.partial(prepare_kernel, per, sub),
        out_shape=jax.ShapeDtypeStruct((steps, ROWS, lanes), BF),
        scratch_shapes=[
            pltpu.VMEM((steps * ROWS, embed.shape[1]), BF),
            pltpu.VMEM((embed.shape[1], 128), BF),
        ],
        compiler_params=params(7),
        name="prepare",
    )(embed, mod_all, w_mine, states, opening)


def attend_kernel(
    heads, n_sub, per, sub, tokd, part_ref, embed_ref, pay_ref, out_ref, queries_ref, keys_scr
):
    chans = embed_ref.shape[0]
    hdim = n_sub * sub
    length = queries_ref.shape[0]
    for source in range(pay_ref.shape[0]):
        last = pay_ref[source, ROWS - 16 :, :].astype(F32)[8:]
        for i in range(tokd // 8):
            start = source * tokd + i * 8
            keys_scr[start : start + 8, :] = last[:, i * chans : (i + 1) * chans]
    first = pl.multiple_of(part_ref[0] * length, length)

    def augmented(p):
        residual = dot(p.astype(BF), embed_ref[...])
        residual = residual - jnp.mean(residual, axis=1, keepdims=True)
        variance = jnp.mean(residual * residual, axis=1, keepdims=True)
        lane = lax.broadcasted_iota(jnp.int32, p.shape, 1)
        return jnp.concatenate([p * lax.rsqrt(variance + 1e-6), (lane == 0).astype(F32)], axis=1)

    every = augmented(keys_scr[...])
    queries = keys_scr[pl.ds(first, length), :]
    queries_ref[...] = queries.astype(BF)
    mine = every if length == keys_scr.shape[0] else augmented(queries)
    keys = every[:, :chans].astype(BF)
    every_t = every.T[: chans + 16].astype(BF)
    products, values = [], []
    for h in range(heads):
        product = None
        value_parts = []
        for j in range(n_sub):
            source, slot = divmod(h * n_sub + j, per)
            part = pay_ref[source, :, slot * chans : (slot + 1) * chans].astype(F32)
            product = part if product is None else product + part
            start = per * chans + slot * sub
            value_parts.append(pay_ref[source, :, start : start + sub])
        products.append(product.astype(BF))
        values.append(jnp.concatenate(value_parts, axis=1) if n_sub > 1 else value_parts[0])
    factor = hdim**-0.5 * math.log2(math.e)
    sides = (dot(mine[:, :ROWS].astype(BF), jnp.concatenate(products, axis=1)) * factor).astype(BF)

    def scores(h):
        return dot(keys, sides[:, h * chans : (h + 1) * chans], ((1,), (1,)))

    mixed = []
    now = scores(0)
    for h in range(heads):
        following = scores(h + 1) if h + 1 < heads else None
        weights = jnp.exp2(now - jnp.max(now, axis=0, keepdims=True)).astype(BF)
        rows = dot(every_t, weights)
        mixed.append(rows * (1.0 / rows[chans : chans + 1]))
        now = following
    for h in range(heads):
        result = dot(mixed[h].T.astype(BF), values[h])
        out_ref[:, h * hdim : (h + 1) * hdim] = result.astype(BF)


def attend(part, embed, payload, tokd, share, heads, n_sub, per, sub):
    length = payload.shape[0] * tokd
    return pl.pallas_call(
        functools.partial(attend_kernel, heads, n_sub, per, sub, tokd),
        out_shape=[
            jax.ShapeDtypeStruct((length // share, heads * n_sub * sub), BF),
            jax.ShapeDtypeStruct((length // share, embed.shape[0]), BF),
        ],
        in_specs=[SMEM, VMEM, VMEM],
        scratch_shapes=[pltpu.VMEM((length, embed.shape[0]), F32)],
        compiler_params=params(7 if share == 1 else 40),
        name="attend",
    )(part, embed, payload)


def finish_kernel(
    tokd, owner_ref, coef_ref, embed_ref, queries_ref, att_ref, gate_ref, final_ref, *refs
):
    *wo_refs, out_ref, wo_scr, sum_scr, sem = refs
    width = wo_scr.shape[1]
    chunk = width // 2
    copies = []
    for c in range(2):
        lanes = pl.ds(c * chunk, chunk)
        for i, ref in enumerate(wo_refs):
            rows = ref.shape[0]
            start = pl.multiple_of(owner_ref[i] * rows, rows)
            target = wo_scr.at[pl.ds(start, rows), lanes]
            copies.append(pltpu.make_async_copy(ref.at[:, lanes], target, sem.at[c, i]))
            copies[-1].start()
    total = 0.0
    for c in range(2):
        lanes = slice(c * chunk, (c + 1) * chunk)
        residual = dot(queries_ref[...], embed_ref[:, lanes])
        for copy in copies[c * len(wo_refs) : (c + 1) * len(wo_refs)]:
            copy.wait()
        updated = residual + gate_ref[:, lanes] * dot(att_ref[...], wo_scr[:, lanes])
        sum_scr[:, lanes] = updated
        total = total + jnp.sum(updated, axis=1, keepdims=True)
    centred = sum_scr[...] - total * (1.0 / width)
    variance = jnp.mean(centred * centred, axis=1, keepdims=True)
    normed = centred * lax.rsqrt(variance + 1e-6)
    high = normed.astype(BF)
    noise = dot(high, final_ref[...], ((1,), (1,)))
    noise = noise * coef_ref[0]
    half = tokd // 2
    for i in range(out_ref.shape[1]):
        block = noise[i * tokd : (i + 1) * tokd]
        block = jnp.concatenate([block[:half], block[half:]], axis=1).astype(BF)
        for j in range(out_ref.shape[0]):
            out_ref[j, i] = block


def finish(owners, coef, embed, queries, att, gate, final, parts, tokd, repeats):
    chans, width = final.shape
    length = queries.shape[0]
    return pl.pallas_call(
        functools.partial(finish_kernel, tokd),
        out_shape=jax.ShapeDtypeStruct((repeats, length // tokd, tokd // 2, 2 * chans), BF),
        in_specs=[SMEM] * 2 + [VMEM] * 5 + [pl.BlockSpec(memory_space=pl.ANY)] * len(parts),
        scratch_shapes=[
            pltpu.VMEM((att.shape[1], width), BF),
            pltpu.VMEM((length, width), F32),
            pltpu.SemaphoreType.DMA((2, len(parts))),
        ],
        compiler_params=params(12),
        name="finish",
    )(owners, coef, embed, queries, att, gate, final, *parts)


def advance_kernel(share, place_ref, keep_ref, noise_ref, states_ref, opening_ref, first_ref, kept_ref, out_ref, square_ref, packed_scr):
    groups, count = noise_ref.shape[:2]
    steps, tokd, chans = states_ref.shape
    packed_scr[...] = jnp.zeros(packed_scr.shape, F32)
    for group in range(groups - 1):

        @pl.when(place_ref[0] > group)
        def _add(group=group):
            total = noise_ref[group, 0].astype(F32)
            for i in range(1, count):
                total = total + noise_ref[group, i].astype(F32)
            packed_scr[...] += total

    def unpack(x):
        return jnp.concatenate([x[:, :chans], x[:, chans:]], axis=0)

    state = first_ref[...] + kept_ref[...] + unpack(packed_scr[...])
    for t in range(steps):
        noise = noise_ref[place_ref[0], t * share].astype(F32)
        for i in range(1, share):
            noise = noise + noise_ref[place_ref[0], t * share + i].astype(F32)
        before = opening_ref[...] if t == 0 else states_ref[t - 1]
        state = state + (keep_ref[t] * before + unpack(noise))
        out_ref[t] = state
        error = state - states_ref[t]
        square_ref[t : t + 1, :] = jnp.sum(error * error, axis=0, keepdims=True)


def advance(place, keep, noise, states, opening, first, kept, share):
    steps, _, chans = states.shape
    return pl.pallas_call(
        functools.partial(advance_kernel, share),
        out_shape=[
            jax.ShapeDtypeStruct(states.shape, F32),
            jax.ShapeDtypeStruct((steps, chans), F32),
        ],
        in_specs=[SMEM] * 2 + [VMEM] * 5,
        scratch_shapes=[pltpu.VMEM(noise.shape[2:], F32)],
        compiler_params=params(2),
        name="advance",
    )(place, keep, noise, states, opening, first, kept)


def swap(x, mask, count):
    return lax.ppermute(x, "seq", [(i, i ^ mask) for i in range(count)])


def turn_by_plane(x, count, tm_count, swapped=0):
    pairs = []
    for i in range(tm_count):
        for j in range(count):
            pairs.append((i * count + j, i * count + (j ^ (4 if (i + j + swapped) % 2 else 2))))
    return lax.ppermute(x, ("tm", "seq"), pairs)


def earlier_total(total, count):
    place = lax.axis_index("tm")
    carried = jnp.zeros_like(total)
    for by in range(1, count):
        carried += lax.ppermute(total, "tm", [(i, i + by) for i in range(count - by)])
    return carried


def total_over_seq(part, count):
    if count != 8:
        return lax.psum(part, "seq")
    part = part + swap(part, 1, count)
    return part + swap(part, 2, count) + swap(part, 4, count) + swap(part, 6, count)


def per_device(
    states,
    first_state,
    now_step,
    next_step,
    embed_weight,
    mod_weight,
    qkv_weight,
    out_weight,
    final_weight,
):
    steps, tokd, chans = states.shape
    count = lax.axis_size("seq")
    tm_count = lax.axis_size("tm")
    time_index = lax.axis_index("tm")
    seq_index = lax.axis_index("seq")
    rows, heads, width_three = qkv_weight.shape
    hdim = width_three // 3
    width = heads * hdim
    share = count // steps
    n_sub = count // math.gcd(count, heads)
    per = heads * n_sub // count
    sub = hdim // n_sub
    barrier = lax.optimization_barrier
    mine = seq_index // share
    part = seq_index % share

    w_sent = cut(jnp.transpose(qkv_weight, (1, 0, 2)), count, n_sub, per, sub)
    w_mine = lax.all_to_all(w_sent, "seq", 0, 0, tiled=True)

    by_planes = count == 8 and tm_count % 2 == 0
    if by_planes:
        first = turn_by_plane(out_weight, count, tm_count)
    late_states, _ = barrier((states, w_sent))
    edge = lax.ppermute(late_states[-1], "tm", [(i, i + 1) for i in range(tm_count - 1)])
    opening = jnp.where(time_index == 0, first_state, edge)
    keep_coef, noise_coef = coefficients(now_step, next_step)
    kept = keep_coef[0] * opening + jnp.sum(keep_coef[1:, None, None] * states[:-1], axis=0)
    kept = earlier_total(kept, tm_count)
    mod_all = modulation(now_step, mod_weight)
    gate = lax.dynamic_slice(mod_all, (mine, 2 * width), (1, width))
    coef = lax.dynamic_slice(noise_coef, (mine,), (1,))
    if by_planes:
        late_first, _ = barrier((first, opening))
        second = lax.ppermute(late_first, "tm", [(i, i ^ 1) for i in range(tm_count)])
    w_mine, mod_all, opening, kept, gate, coef = barrier((w_mine, mod_all, opening, kept, gate, coef))
    if by_planes:
        late_first, _ = barrier((first, w_mine))
        third = turn_by_plane(late_first, count, tm_count, 1)

    payload = prepare(embed_weight, mod_all, w_mine, states, opening, per, sub)
    sent = jnp.repeat(payload, share, axis=0)
    received = lax.all_to_all(sent, "seq", 0, 0, tiled=True)
    if by_planes:
        own, first, second, _ = barrier((out_weight, first, second, payload))
        third, _ = barrier((third, received))
        parts = []
        for block in (own, first, second, third):
            parts += [block, swap(block, 1, count)]
        one = jnp.where((seq_index + time_index) % 2 == 0, 2, 4)
        two = 6 - one
        zero = jnp.zeros_like(one)
        owners = [zero, zero + 1, one, two + 1, two, one + 1, zero + 6, zero + 7]
        owners = seq_index ^ jnp.stack(owners)
    else:
        parts = [lax.all_gather(out_weight, "seq", axis=0, tiled=True)]
        owners = jnp.zeros((1,), jnp.int32)
    part_place = jnp.full((1,), part, jnp.int32)
    att, queries = attend(part_place, embed_weight, received, tokd, share, heads, n_sub, per, sub)
    repeats = tm_count if share == 1 else 1
    noise = finish(
        owners, coef, embed_weight, queries, att, gate, final_weight.T, parts, tokd, repeats
    )

    if share > 1:
        full = jnp.zeros((share,) + noise.shape[1:], BF)
        full = lax.dynamic_update_slice(full, noise, (part, 0, 0, 0))
        noise = jnp.broadcast_to(full[None], (tm_count,) + full.shape)
    block = noise.shape[-2:]
    noise = noise.reshape((tm_count * count,) + block)
    noise = lax.all_to_all(noise, ("tm", "seq"), 0, 0, tiled=True)
    noise = noise.reshape((tm_count, count) + block)
    time_place = jnp.full((1,), time_index, jnp.int32)
    advanced, squares = advance(time_place, keep_coef, noise, states, opening, first_state, kept, share)
    errors = jnp.sum(total_over_seq(squares, count), axis=1) / (tokd * count * chans)
    return (advanced, errors)


def solution(mesh):
    in_specs = (
        P("tm", "seq", None),
        P("seq", None),
        P("tm"),
        P("tm"),
        P(),
        P(),
        P("seq", None, None),
        P("seq", None),
        P(),
    )
    out_specs = (P("tm", "seq", None), P("tm"))
    return jax.shard_map(
        per_device, mesh=mesh, in_specs=in_specs, out_specs=out_specs, check_vma=False
    )
```
